512 devices in a mesh: blk: 128 (over z, y, x_lo), vox: 4 (over x_hi, core).
Axes of the slice: x: 4 (x_hi: 2, x_lo: 2; x = x_hi * 2 + x_lo), y: 4, z: 16, core: 2. Of those that a mesh axis runs over, the one named last changes fastest.
Arguments:
- particles: bfloat16 [24576, 2, 5120], P('blk', None, 'vox'), may hold values from -6 to 6
- classes: int32 [24576], P('blk'), may hold values from 0 to 7
- plan: int32 [2, 128], replicated, may hold values from 0 to 127, as said below
- voxel_shell: int32 [5120], P('vox'), may hold values from 4 to 16
- voxel_angle: int32 [5120], P('vox'), may hold values from 0 to 89
- shell_gain: float32 [13], replicated, may hold values from 0.25 to 4
Outputs:
- significance: float32 [3, 24576, 192], P(None, 'blk', 'vox')
The draws below stay inside these ranges and needn't reach their ends.
Inputs may be any that keep to these rules, and one draw needn't show every extreme that they name: In round r every block b meets block plan[r, b] = b XOR 2^k, with one k a round and different k in different rounds; every block is its partner's partner.
All inputs are finite; a program needn't handle non-finite values.
Results may differ from the reference program's by a relative error of at most 0.0013.
Values may be sent and summed in bfloat16 or wider, within the bound.
No kernel may reach another device: no remote copies, remote signals or barrier semaphores. Data moves between devices by JAX's collectives and lax.ppermute only.
A program may use at most 64 MiB of HBM per device.

```python
import math
import jax
import jax.numpy as jnp
from jax import lax

VOX = 5120
CLASSES = 8
SHELLS = 13
ROUNDS = 2
BLOCK = 192
PARTICLES = 24576
SLOTS = 3
N_BLK = 128


def draw_plan(key, part):
    key = jax.random.fold_in(key, 7)
    bit_count = N_BLK.bit_length() - 1
    exponents = jax.random.permutation(key, bit_count)[:ROUNDS].astype(jnp.int32)
    blocks = jnp.arange(N_BLK, dtype=jnp.int32)
    return jnp.bitwise_xor(blocks[None, :], jnp.left_shift(jnp.int32(1), exponents)[:, None]).astype(jnp.int32)


def set_ends(values, stream_key, least, high):
    longest = values.shape.index(max(values.shape))
    spots = []
    for shift in (0, 1):
        where = [jax.random.randint(jax.random.fold_in(stream_key, axis), (), 0, length) for axis, length in enumerate(values.shape)]
        where[longest] = (where[longest] + shift) % values.shape[longest]
        spots.append(tuple(where))
    return values.at[spots[0]].set(least).at[spots[1]].set(high)


def level_of(own_key, extent, pieces, smallest, largest):
    loudness = 1.0
    for position, parts in pieces:
        steps = jax.random.uniform(jax.random.fold_in(jax.random.fold_in(own_key, 6), position), (parts,), jnp.float32, smallest / len(pieces), largest / len(pieces))
        loudness = loudness * jnp.repeat(jnp.exp(steps), extent[position] // parts).reshape((-1,) + (1,) * (len(extent) - 1 - position))
    return loudness


def gaussian(rng, shape, spread, most, split=(), kind=jnp.bfloat16):
    values = jax.random.normal(rng, shape, jnp.float32) * spread
    if len(split) > 0:
        values = level_of(rng, shape, split, -0.22, 0.18) * values
    return jnp.clip(values, min=-most, max=most).astype(kind)


def setup_inputs(seed: int = 0) -> dict:
    key_of = jax.random.split(jax.random.key(seed), 7)
    particles = gaussian(key_of[0], (PARTICLES, 2, VOX), 1.0, 6.0, ((0, 128), (2, 4)))
    classes = set_ends(jax.random.randint(key_of[1], (PARTICLES,), 0, CLASSES), jax.random.fold_in(key_of[1], 1), 0, CLASSES - 1).astype(jnp.int32)
    plan = draw_plan(jax.random.fold_in(key_of[6], 71), 0)
    voxel_shell = set_ends(jax.random.randint(key_of[3], (VOX,), 4, 17), jax.random.fold_in(key_of[3], 1), 4, 16).astype(jnp.int32)
    voxel_angle = set_ends(jax.random.randint(key_of[4], (VOX,), 0, 90), jax.random.fold_in(key_of[4], 1), 0, 89).astype(jnp.int32)
    shell_gain = jnp.clip(jnp.exp(jax.random.uniform(key_of[5], (SHELLS,), jnp.float32, math.log(0.25), math.log(4.0))), 0.25, 4.0)
    return dict(particles=particles, classes=classes, plan=plan, voxel_shell=voxel_shell, voxel_angle=voxel_angle, shell_gain=shell_gain)


first_shell = 4
epsilon = 1e-05

def tables(voxel_shell, voxel_angle, shell_gain):
    limits = 48 + 3 * jnp.arange(8, dtype=jnp.int32)
    mask_table = (voxel_angle[None, :] <= limits[:, None]).astype(jnp.float32)
    shells = first_shell + jnp.arange(shell_gain.shape[0], dtype=jnp.int32)
    weights = lax.optimization_barrier(jnp.sum(jnp.where(voxel_shell[None, :] == shells[:, None], shell_gain[:, None], jnp.float32(0.0)), axis=0))
    weight_table = (mask_table * weights[None, :]).astype(jnp.bfloat16)
    return (mask_table, weight_table)

def contract(left_side, right_side):
    return lax.dot_general(left_side, right_side, (((1,), (1,)), ((), ())), preferred_element_type=jnp.float32)

def slot_scores(own_block, own_cls, other_block, other_cls, mask_table, weight_table):
    row_count = own_block.shape[0]
    own_mask = mask_table[own_cls]
    other_mask = mask_table[other_cls]
    other_weights = weight_table[other_cls].astype(jnp.float32)
    own_wide = own_block.astype(jnp.float32)
    other_wide = other_block.astype(jnp.float32)
    masked = (own_wide * own_mask[:, None, :]).astype(jnp.bfloat16)
    weighted = (other_wide * other_weights[:, None, :]).astype(jnp.bfloat16)
    score_sum = contract(masked.reshape(row_count, -1), weighted.reshape(row_count, -1))
    own_power = (lax.optimization_barrier(jnp.sum(own_wide * own_wide, axis=1)) * own_mask).astype(jnp.bfloat16)
    other_power = (lax.optimization_barrier(jnp.sum(other_wide * other_wide, axis=1)) * other_mask).astype(jnp.bfloat16)
    own_table = contract(own_power, weight_table)
    other_table = contract(other_power, weight_table)
    labels = jnp.arange(8, dtype=jnp.int32)
    onehot_own = (own_cls[:, None] == labels[None, :]).astype(jnp.float32)
    onehot_other = (other_cls[:, None] == labels[None, :]).astype(jnp.float32)
    left_norm = jnp.dot(own_table, onehot_other.T, precision=lax.Precision.HIGHEST)
    right_norm = jnp.dot(onehot_own, other_table.T, precision=lax.Precision.HIGHEST)
    voxel_total = VOX
    return score_sum / math.sqrt(voxel_total) * lax.rsqrt((left_norm / voxel_total + epsilon) * (right_norm / voxel_total + epsilon))

def reference(particles, classes, plan, voxel_shell, voxel_angle, shell_gain):
    mask_table, weight_table = tables(voxel_shell, voxel_angle, shell_gain)
    block_view = particles.reshape(N_BLK, BLOCK, 2, VOX)
    class_view = classes.reshape(N_BLK, BLOCK)
    blocks = jnp.arange(N_BLK, dtype=jnp.int32)
    partners = jnp.concatenate([blocks[None, :], plan.astype(jnp.int32)], axis=0).reshape(-1)
    owners = jnp.tile(blocks, SLOTS)

    def one_pair(pair_ids):
        owner, partner = pair_ids
        return slot_scores(block_view[owner], class_view[owner], block_view[partner], class_view[partner], mask_table, weight_table)
    result = lax.map(one_pair, (owners, partners))
    return result.reshape(SLOTS, PARTICLES, BLOCK)
```

```python
import math

import jax
import jax.numpy as jnp
from jax import lax
from jax.experimental import pallas as pl
from jax.experimental.pallas import tpu as pltpu
from jax.sharding import PartitionSpec as P

first_shell = 4
first_limit = 48
limit_step = 3
class_count = 8
epsilon = 1e-05

f32 = jnp.float32
bf16 = jnp.bfloat16
in_vmem = pl.BlockSpec(memory_space=pltpu.VMEM)
in_smem = pl.BlockSpec(memory_space=pltpu.SMEM)


def shape(dims, dtype):
    return jax.ShapeDtypeStruct(dims, dtype)


def local_call(kernel, out_shape, in_specs, out_specs, args, flops=0, size=0):
    return pl.pallas_call(
        kernel,
        out_shape=out_shape,
        in_specs=in_specs,
        out_specs=out_specs,
        compiler_params=pltpu.CompilerParams(vmem_limit_bytes=40 << 20),
        cost_estimate=pl.CostEstimate(flops=flops, bytes_accessed=size, transcendentals=0),
    )(*args)


def contract(left_side, right_side):
    return lax.dot_general(
        left_side, right_side, (((1,), (1,)), ((), ())), preferred_element_type=f32
    )


def one_way(blocks, voxes, bit):
    return [
        (b * voxes + v, (b ^ 1 << bit) * voxes + v)
        for b in range(blocks)
        for v in range(voxes)
        if v & 1 == b >> bit & 1
    ]


def back(pairs):
    return [(target, source) for source, target in pairs]


def both_ways(blocks, bit):
    return [(b, b ^ 1 << bit) for b in range(blocks)]


def branch_kernel(bit_count, plan, index_out, flag_out):
    first, second = plan[0, 0], plan[1, 0]

    def bit_of(value):
        return sum([jnp.where(value >= 1 << k, 1, 0) for k in range(1, bit_count)])

    first, second = bit_of(first), bit_of(second)
    low, high = jnp.minimum(first, second), jnp.maximum(first, second)
    index_out[0] = high * (high - 1) // 2 + low
    flag_out[0] = jnp.where(first > second, 1, 0)


def column(row):
    return jnp.broadcast_to(row, (8, row.shape[1])).T[:, 0:1]


def keep_rows(labels, angles):
    limits = first_limit + 1.0 + limit_step * column(labels.astype(f32))
    return jnp.clip(limits.astype(bf16) - angles, 0, 1)


def own_kernel(gain, x, labels, shells, angles, left_out, right_out, message, rows):
    count = x.shape[0]
    weights = jnp.zeros(shells.shape, f32)
    for s in range(gain.shape[0]):
        weights = jnp.where(shells[...] == s + first_shell, gain[s], weights)
    weights = weights.astype(bf16)
    angle_row = angles[...].astype(f32)
    rows[0:1, :] = weights.astype(f32)
    rows[1:2, :] = angle_row
    keep = keep_rows(labels[...], angle_row.astype(bf16))
    limits = first_limit + limit_step * lax.broadcasted_iota(jnp.int32, (class_count, 1), 0)
    table = jnp.where(angles[...] <= limits, weights.astype(f32), 0.0).astype(bf16)
    block = x[...]
    left = [block[:, t, :] * keep for t in range(2)]
    right = [part * weights for part in left]
    wide = [part.astype(f32) for part in left]
    power = (wide[0] * wide[0] + wide[1] * wide[1]).astype(bf16)
    table_sums = contract(table, power)
    scores = contract(right[0], left[0]) + contract(right[1], left[1])
    for t in range(2):
        left_out[t] = left[t]
        right_out[t] = right[t]
    parts, height = message.shape[0], message.shape[1] - class_count
    for q in range(parts):
        message[q, 0:height, :] = scores[height * q : height * (q + 1), :]
        message[q, height:, :] = table_sums


def norms(own_sums, own_labels, slice_sums, slice_labels, total):
    left_norm = jnp.zeros((slice_sums.shape[0], own_sums.shape[1]), f32)
    right_norm = left_norm
    for c in range(class_count):
        left_norm = jnp.where(slice_labels == c, own_sums[c : c + 1, :], left_norm)
        right_norm = jnp.where(own_labels == c, slice_sums[:, c : c + 1], right_norm)
    return lax.rsqrt((left_norm / total + epsilon) * (right_norm / total + epsilon)) / math.sqrt(
        total
    )


def sliced(place, height, sums, labels, scratch):
    scratch[:, 0:class_count] = sums.T
    scratch[:, class_count : 2 * class_count] = jnp.broadcast_to(
        labels.astype(f32), (class_count, labels.shape[1])
    ).T
    part = scratch[pl.ds(pl.multiple_of(place[0] * height, 8), height), :]
    return part[:, 0:class_count], part[:, class_count : class_count + 1]


def self_kernel(total, place, message, labels, sums_out, out, scratch):
    height = message.shape[1] - class_count
    summed = message[0]
    for q in range(1, message.shape[0]):
        summed = summed + message[q]
    sums = summed[height:, :]
    sums_out[...] = sums
    slice_sums, slice_labels = sliced(place, height, sums, labels[...], scratch)
    factors = norms(sums, labels[...].astype(f32), slice_sums, slice_labels, total)
    out[...] = summed[0:height, :] * factors


def factor_kernel(total, place, sums, labels, *refs):
    others, out, scratch = refs[:-2], refs[-2], refs[-1]
    count = sums.shape[1]
    height = out.shape[0]
    own_labels = labels[...].astype(f32)
    for s in range(len(others) // 2):
        slice_sums, slice_labels = sliced(
            place, height, others[2 * s][...], others[2 * s + 1][...], scratch
        )
        out[:, count * s : count * (s + 1)] = norms(
            sums[...], own_labels, slice_sums, slice_labels, total
        )


def pair_kernel(x, labels, rows, left, right, own_out, send_out):
    weights = rows[0:1, :].astype(bf16)
    keep = keep_rows(labels[...], rows[1:2, :].astype(bf16))
    block = x[...]
    part = [block[:, t, :] * keep for t in range(2)]
    own_out[...] = contract(part[0] * weights, left[0]) + contract(part[1] * weights, left[1])
    sent = contract(right[0], part[0]) + contract(right[1], part[1])
    half, count = send_out.shape[0], sent.shape[1]
    send_out[:, 0:count] = sent[0:half]
    send_out[:, count:] = sent[half:]


def merge_kernel(*refs):
    out = refs[-1]
    parts, height = out.shape[0], out.shape[1]
    for s in range((len(refs) - 1) // 2):
        own, received = refs[2 * s], refs[2 * s + 1]
        half, count = received.shape[0], own.shape[1]
        for q in range(parts):
            side, at = divmod(q * height, half)
            out[q, :, count * s : count * (s + 1)] = (
                own[height * q : height * (q + 1), :]
                + received[at : at + height, count * side : count * (side + 1)]
            )


def last_kernel(flag, pieces, factors, first_out, out):
    count = out.shape[2]
    summed = pieces[0]
    for q in range(1, pieces.shape[0]):
        summed = summed + pieces[q]
    summed = summed * factors[...]
    out[0] = first_out[...]
    for s in range(out.shape[0] - 1):
        out[1 + (s ^ flag[0])] = summed[:, count * s : count * (s + 1)]


def rounds(bits, blocks, voxes, x, labels, shells, angles, gain, place, flag):
    count, _, width = x.shape
    height = count // voxes
    total = width * voxes
    axes = ("blk", "vox")
    labels = labels.reshape(1, -1)
    received = [lax.ppermute(x, axes, one_way(blocks, voxes, bit)) for bit in bits]
    other_labels = [lax.ppermute(labels, "blk", both_ways(blocks, bit)) for bit in bits]
    left, right, message, rows = local_call(
        own_kernel,
        (
            shape((2, count, width), bf16),
            shape((2, count, width), bf16),
            shape((voxes, height + class_count, count), f32),
            shape((8, width), f32),
        ),
        [in_smem] + [in_vmem] * 4,
        (in_vmem,) * 4,
        (gain, x, labels, shells.reshape(1, -1), angles.reshape(1, -1)),
        flops=6 * count * count * width,
        size=12 << 20,
    )
    message = lax.all_to_all(message, "vox", 0, 0, tiled=True)

    def self_call(*refs):
        self_kernel(total, *refs)

    def factor_call(*refs):
        factor_kernel(total, *refs)

    scratch = [pltpu.VMEM((count, 2 * class_count), f32)]
    params = pltpu.CompilerParams(vmem_limit_bytes=40 << 20)
    sums, first_out = pl.pallas_call(
        self_call,
        out_shape=(shape((class_count, count), f32), shape((height, count), f32)),
        in_specs=[in_smem, in_vmem, in_vmem],
        out_specs=(in_vmem, in_vmem),
        scratch_shapes=scratch,
        compiler_params=params,
        cost_estimate=pl.CostEstimate(flops=0, bytes_accessed=3 << 20, transcendentals=0),
    )(place, message, labels)
    rows, sums = lax.optimization_barrier((rows, sums))
    other_sums = [lax.ppermute(sums, "blk", both_ways(blocks, bit)) for bit in bits]
    factors = pl.pallas_call(
        factor_call,
        out_shape=shape((height, len(bits) * count), f32),
        in_specs=[in_smem] + [in_vmem] * (2 + 2 * len(bits)),
        out_specs=in_vmem,
        scratch_shapes=scratch,
        compiler_params=params,
        cost_estimate=pl.CostEstimate(flops=0, bytes_accessed=3 << 20, transcendentals=0),
    )(place, sums, labels, *[a for pair in zip(other_sums, other_labels) for a in pair])
    sides = []
    for s in range(len(bits)):
        own, sent = local_call(
            pair_kernel,
            (shape((count, count), f32), shape((count // 2, 2 * count), f32)),
            [in_vmem] * 5,
            (in_vmem, in_vmem),
            (received[s], other_labels[s], rows, left, right),
            flops=8 * count * count * width,
            size=10 << 20,
        )
        sides += [own, lax.ppermute(sent, axes, back(one_way(blocks, voxes, bits[s])))]
    merged = local_call(
        merge_kernel,
        shape((voxes, height, len(bits) * count), f32),
        [in_vmem] * len(sides),
        in_vmem,
        sides,
        size=2 << 20,
    )
    pieces = lax.all_to_all(merged, "vox", 0, 0, tiled=True)
    return local_call(
        last_kernel,
        shape((1 + len(bits), height, count), f32),
        [in_smem] + [in_vmem] * 3,
        in_vmem,
        (flag, pieces, factors, first_out),
        size=2 << 20,
    )


def body(particles, classes, plan, voxel_shell, voxel_angle, shell_gain):
    blocks, voxes = lax.axis_size("blk"), lax.axis_size("vox")
    bit_count = blocks.bit_length() - 1

    def branch_call(*refs):
        branch_kernel(bit_count, *refs)

    index, flag = local_call(
        branch_call,
        (shape((1,), jnp.int32), shape((1,), jnp.int32)),
        [in_smem],
        (in_smem, in_smem),
        (plan,),
    )
    place = lax.axis_index("vox").reshape(1)

    def branch(bits):
        return lambda *args: rounds(bits, blocks, voxes, *args)

    out = lax.switch(
        index[0],
        [branch((low, high)) for high in range(bit_count) for low in range(high)],
        particles,
        classes,
        voxel_shell,
        voxel_angle,
        shell_gain,
        place,
        flag,
    )
    return out.transpose(0, 2, 1)


def solution(mesh):
    in_specs = (P("blk", None, "vox"), P("blk"), P(), P("vox"), P("vox"), P())
    out_specs = P(None, "blk", "vox")
    return jax.shard_map(body, mesh=mesh, in_specs=in_specs, out_specs=out_specs, check_vma=False)
```

```python
import math

import jax
import jax.numpy as jnp
from jax import lax
from jax.experimental import pallas as pl
from jax.experimental.pallas import tpu as pltpu
from jax.sharding import PartitionSpec as P

first_shell = 4
first_limit = 48
limit_step = 3
class_count = 8
epsilon = 1e-05

f32 = jnp.float32
bf16 = jnp.bfloat16
in_vmem = pl.BlockSpec(memory_space=pltpu.VMEM)
in_smem = pl.BlockSpec(memory_space=pltpu.SMEM)


def shape(dims, dtype):
    return jax.ShapeDtypeStruct(dims, dtype)


def local_call(kernel, out_shape, in_specs, out_specs, args, scratch=()):
    return pl.pallas_call(
        kernel,
        out_shape=out_shape,
        in_specs=in_specs,
        out_specs=out_specs,
        scratch_shapes=scratch,
        compiler_params=pltpu.CompilerParams(vmem_limit_bytes=40 << 20),
    )(*args)


def contract(left_side, right_side):
    return lax.dot_general(
        left_side, right_side, (((1,), (1,)), ((), ())), preferred_element_type=f32
    )


def one_way(blocks, voxes, bit):
    return [
        (b * voxes + v, (b ^ 1 << bit) * voxes + v)
        for b in range(blocks)
        for v in range(voxes)
        if v & 1 == b >> bit & 1
    ]


def back(pairs):
    return [(target, source) for source, target in pairs]


def both_ways(blocks, bit):
    return [(b, b ^ 1 << bit) for b in range(blocks)]


def branch_kernel(bit_count, plan, index_out, flag_out):
    first, second = plan[0, 0], plan[1, 0]

    def bit_of(value):
        return sum([jnp.where(value >= 1 << k, 1, 0) for k in range(1, bit_count)])

    first, second = bit_of(first), bit_of(second)
    low, high = jnp.minimum(first, second), jnp.maximum(first, second)
    index_out[0] = high * (high - 1) // 2 + low
    flag_out[0] = jnp.where(first > second, 1, 0)


def column(row):
    return jnp.broadcast_to(row, (8, row.shape[1])).T[:, 0:1]


def limits_of(labels):
    return first_limit + 1.0 + limit_step * column(labels.astype(f32))


def chunk_of(width):
    return next(size for size in (256, 128, width) if width % size == 0)


def own_kernel(gain, x, labels, shells, angles, left_out, right_out, rows, partial, message, acc):
    chunk = chunk_of(x.shape[2])
    limits = first_limit + limit_step * lax.broadcasted_iota(jnp.int32, (class_count, 1), 0)
    keep_limits = (limits_of(labels[...])).astype(bf16)
    acc[...] = jnp.zeros(acc.shape, f32)
    partial[0:class_count, :] = jnp.zeros((class_count, partial.shape[1]), f32)

    def step(i, carry):
        at = pl.ds(pl.multiple_of(i * chunk, chunk), chunk)
        weights = jnp.zeros((1, chunk), f32)
        for s in range(gain.shape[0]):
            weights = jnp.where(shells[:, at] == s + first_shell, gain[s], weights)
        weights = weights.astype(bf16)
        rows[0:1, at] = weights.astype(f32)
        table = jnp.where(angles[:, at] <= limits, weights.astype(f32), 0.0).astype(bf16)
        keep = jnp.clip(keep_limits - angles[:, at].astype(f32).astype(bf16), 0, 1)
        block = x[:, :, at]
        left = [block[:, t, :] * keep for t in range(2)]
        right = [part * weights for part in left]
        wide = [part.astype(f32) for part in left]
        power = (wide[0] * wide[0] + wide[1] * wide[1]).astype(bf16)
        partial[0:class_count, :] += contract(table, power)
        for t in range(2):
            left_out[t, :, at] = left[t]
            right_out[t, :, at] = right[t]
        acc[...] += contract(right[0], left[0]) + contract(right[1], left[1])
        return carry

    lax.fori_loop(0, x.shape[2] // chunk, step, 0)
    partial[class_count:, :] = jnp.broadcast_to(
        labels[...].astype(f32), (class_count, partial.shape[1])
    )
    parts, height = message.shape[0], message.shape[1] - class_count
    for q in range(parts):
        message[q, 0:height, :] = acc[height * q : height * (q + 1), :]
        message[q, height:, :] = partial[0:class_count, :]


def norms(own_sums, own_labels, slice_sums, slice_labels, total):
    left_norm = jnp.zeros((slice_sums.shape[0], own_sums.shape[1]), f32)
    right_norm = left_norm
    for c in range(class_count):
        left_norm = jnp.where(slice_labels == c, own_sums[c : c + 1, :], left_norm)
        right_norm = jnp.where(own_labels == c, slice_sums[:, c : c + 1], right_norm)
    return lax.rsqrt((left_norm / total + epsilon) * (right_norm / total + epsilon)) / math.sqrt(
        total
    )


def sliced(place, height, sums, labels, scratch):
    scratch[:, 0:class_count] = sums.T
    scratch[:, class_count : 2 * class_count] = jnp.broadcast_to(
        labels, (class_count, labels.shape[1])
    ).T
    part = scratch[pl.ds(pl.multiple_of(place[0] * height, 8), height), :]
    return part[:, 0:class_count], part[:, class_count : class_count + 1]


def summed_of(message):
    summed = message[0]
    for q in range(1, message.shape[0]):
        summed = summed + message[q]
    return summed


def self_kernel(total, place, message, labels, sums_out, out, scratch):
    height = message.shape[1] - class_count
    summed = summed_of(message)
    sums = summed[height:, :]
    sums_out[...] = sums
    own_labels = labels[...].astype(f32)
    slice_sums, slice_labels = sliced(place, height, sums, own_labels, scratch)
    out[...] = summed[0:height, :] * norms(sums, own_labels, slice_sums, slice_labels, total)


def pair_kernel(first, second, rows, left, right, own_out, first_out, second_out, acc):
    chunk = chunk_of(left.shape[2])
    own_out[...] = jnp.zeros(own_out.shape, f32)
    acc[...] = jnp.zeros(acc.shape, f32)

    def step(i, carry):
        at = pl.ds(pl.multiple_of(i * chunk, chunk), chunk)
        weights = rows[0:1, at].astype(bf16)
        for s, block in enumerate((first, second)):
            own_out[s] += contract(block[0, :, at] * weights, left[0, :, at]) + contract(
                block[1, :, at] * weights, left[1, :, at]
            )
            acc[s] += contract(right[0, :, at], block[0, :, at]) + contract(
                right[1, :, at], block[1, :, at]
            )
        return carry

    lax.fori_loop(0, left.shape[2] // chunk, step, 0)
    for s, out in enumerate((first_out, second_out)):
        half, count = out.shape[0], acc.shape[2]
        out[:, 0:count] = acc[s, 0:half, :]
        out[:, count:] = acc[s, half:, :]


def merge_kernel(own, first, second, first_partial, second_partial, out):
    parts, height = out.shape[0], out.shape[1] - class_count
    count = own.shape[2]
    for s, (received, partial) in enumerate(((first, first_partial), (second, second_partial))):
        half = received.shape[0]
        across = slice(count * s, count * (s + 1))
        for q in range(parts):
            side, at = divmod(q * height, half)
            out[q, 0:height, across] = (
                own[s, height * q : height * (q + 1), :]
                + received[at : at + height, count * side : count * (side + 1)]
            )
            out[q, height:, across] = partial[0:class_count, :]


def last_kernel(
    total, flag, place, pieces, sums, labels, first_partial, second_partial, self_out, out, scratch
):
    count, height = out.shape[2], out.shape[1]
    summed = summed_of(pieces)
    own_labels = labels[...].astype(f32)
    out[0] = self_out[...]
    for s, partial in enumerate((first_partial, second_partial)):
        mine = summed[:, count * s : count * (s + 1)]
        slice_sums, slice_labels = sliced(
            place, height, mine[height:, :], partial[class_count : class_count + 1, :], scratch
        )
        out[1 + (s ^ flag[0])] = mine[0:height, :] * norms(
            sums[...], own_labels, slice_sums, slice_labels, total
        )


def body(particles, classes, plan, voxel_shell, voxel_angle, shell_gain):
    blocks, voxes = lax.axis_size("blk"), lax.axis_size("vox")
    bit_count = blocks.bit_length() - 1
    count, _, width = particles.shape
    height, total = count // voxes, width * voxes
    axes = ("blk", "vox")
    bit_pairs = [(low, high) for high in range(bit_count) for low in range(high)]

    def branch_call(*refs):
        branch_kernel(bit_count, *refs)

    def self_call(*refs):
        self_kernel(total, *refs)

    def last_call(*refs):
        last_kernel(total, *refs)

    index, flag = local_call(
        branch_call,
        (shape((1,), jnp.int32), shape((1,), jnp.int32)),
        [in_smem],
        (in_smem, in_smem),
        (plan,),
    )
    index = index[0]
    place = lax.axis_index("vox").reshape(1)
    labels = classes.reshape(1, -1)
    left, right, rows, partial, message = local_call(
        own_kernel,
        (
            shape((2, count, width), bf16),
            shape((2, count, width), bf16),
            shape((8, width), f32),
            shape((2 * class_count, count), f32),
            shape((voxes, height + class_count, count), f32),
        ),
        [in_smem] + [in_vmem] * 4,
        (in_vmem,) * 5,
        (shell_gain, particles, labels, voxel_shell.reshape(1, -1), voxel_angle.reshape(1, -1)),
        [pltpu.VMEM((count, count), f32)],
    )
    message = lax.all_to_all(message, "vox", 0, 0, tiled=True)

    def fetch(bits):
        return lambda block, own_partial: tuple(
            [lax.ppermute(block, axes, one_way(blocks, voxes, bit)) for bit in bits]
            + [lax.ppermute(own_partial, "blk", both_ways(blocks, bit)) for bit in bits]
        )

    def give_back(bits):
        return lambda *sent: tuple(
            lax.ppermute(part, axes, back(one_way(blocks, voxes, bit)))
            for part, bit in zip(sent, bits)
        )

    first, second, first_partial, second_partial = lax.switch(
        index, [fetch(bits) for bits in bit_pairs], left, partial
    )
    scratch = [pltpu.VMEM((count, 2 * class_count), f32)]
    sums, self_out = local_call(
        self_call,
        (shape((class_count, count), f32), shape((height, count), f32)),
        [in_smem, in_vmem, in_vmem],
        (in_vmem, in_vmem),
        (place, message, labels),
        scratch,
    )
    own, first_sent, second_sent = local_call(
        pair_kernel,
        (shape((2, count, count), f32),) + (shape((count // 2, 2 * count), f32),) * 2,
        [in_vmem] * 5,
        (in_vmem,) * 3,
        (first, second, rows, left, right),
        [pltpu.VMEM((2, count, count), f32)],
    )
    first_back, second_back = lax.switch(
        index, [give_back(bits) for bits in bit_pairs], first_sent, second_sent
    )
    merged = local_call(
        merge_kernel,
        shape((voxes, height + class_count, 2 * count), f32),
        [in_vmem] * 5,
        in_vmem,
        (own, first_back, second_back, first_partial, second_partial),
    )
    pieces = lax.all_to_all(merged, "vox", 0, 0, tiled=True)
    out = local_call(
        last_call,
        shape((3, height, count), f32),
        [in_smem, in_smem] + [in_vmem] * 6,
        in_vmem,
        (flag, place, pieces, sums, labels, first_partial, second_partial, self_out),
        scratch,
    )
    return out.transpose(0, 2, 1)


def solution(mesh):
    in_specs = (P("blk", None, "vox"), P("blk"), P(), P("vox"), P("vox"), P())
    out_specs = P(None, "blk", "vox")
    return jax.shard_map(body, mesh=mesh, in_specs=in_specs, out_specs=out_specs, check_vma=False)
```

```python
import math

import jax
import jax.numpy as jnp
from jax import lax
from jax.experimental import pallas as pl
from jax.experimental.pallas import tpu as pltpu
from jax.sharding import PartitionSpec as P

first_shell = 4
first_limit = 48
limit_step = 3
class_count = 8
epsilon = 1e-05
front_vmem = 60 << 20

f32 = jnp.float32
bf16 = jnp.bfloat16
in_vmem = pl.BlockSpec(memory_space=pltpu.VMEM)
in_hbm = pl.BlockSpec(memory_space=pltpu.HBM)
in_smem = pl.BlockSpec(memory_space=pltpu.SMEM)


def shape(dims, dtype):
    return jax.ShapeDtypeStruct(dims, dtype)


def local_call(kernel, out_shape, in_specs, out_specs, args, scratch=(), vmem=40 << 20):
    return pl.pallas_call(
        kernel,
        out_shape=out_shape,
        in_specs=in_specs,
        out_specs=out_specs,
        scratch_shapes=scratch,
        compiler_params=pltpu.CompilerParams(vmem_limit_bytes=vmem),
    )(*args)


def contract(left_side, right_side):
    return lax.dot_general(
        left_side, right_side, (((1,), (1,)), ((), ())), preferred_element_type=f32
    )


def one_way(blocks, voxes, bit):
    return [
        (b * voxes + v, (b ^ 1 << bit) * voxes + v)
        for b in range(blocks)
        for v in range(voxes)
        if v & 1 == b >> bit & 1
    ]


def back(pairs):
    return [(target, source) for source, target in pairs]


def both_ways(blocks, bit):
    return [(b, b ^ 1 << bit) for b in range(blocks)]


def column(row):
    return jnp.broadcast_to(row, (8, row.shape[1])).T[:, 0:1]


def limits_of(labels):
    return first_limit + 1.0 + limit_step * column(labels.astype(f32))


def chunk_of(width):
    return next(size for size in (256, 128, width) if width % size == 0)


def mask_kernel(
    bit_count, x, labels, plan, shells, angles, gain, index_out, flag_out, left_out, *scratch
):
    rows, buffers, sems = scratch[0], scratch[1:-1], scratch[-1]
    half = left_out.shape[1] // 2
    block, labels_in, plan_in, shells_in, angles_in, gain_in = buffers
    halves = [
        pltpu.make_async_copy(
            x.at[pl.ds(half * h, half)], block.at[pl.ds(half * h, half)], sems.at[h]
        )
        for h in range(2)
    ]
    small = [
        pltpu.make_async_copy(source, buffer, sems.at[2 + i])
        for i, (source, buffer) in enumerate(
            zip((labels, plan, shells, angles, gain), buffers[1:])
        )
    ]
    for copy in small + halves:
        copy.start()
    for copy in small:
        copy.wait()

    def bit_of(value):
        return sum([jnp.where(value >= 1 << k, 1, 0) for k in range(1, bit_count)])

    first, second = bit_of(plan_in[0, 0]), bit_of(plan_in[1, 0])
    low, high = jnp.minimum(first, second), jnp.maximum(first, second)
    index_out[0] = high * (high - 1) // 2 + low
    flag_out[0] = jnp.where(first > second, 1, 0)

    shell_row = shells_in[...].reshape(1, -1)
    angle_row = angles_in[...].reshape(1, -1).astype(f32)
    weights = jnp.zeros(shell_row.shape, f32)
    for s in range(gain.shape[0]):
        weights = jnp.where(shell_row == s + first_shell, gain_in[s], weights)
    rows[0:1, :] = weights.astype(bf16).astype(f32)
    rows[1:2, :] = angle_row
    limits = limits_of(labels_in[...].reshape(1, -1)).astype(bf16)
    chunk = chunk_of(x.shape[2])
    for h in range(2):
        halves[h].wait()

        def step(i, carry):
            at = pl.ds(pl.multiple_of(i * chunk, chunk), chunk)
            keep = jnp.clip(
                limits[half * h : half * (h + 1)] - rows[1:2, at].astype(bf16), 0, 1
            )
            parts = jnp.swapaxes(block[half * h : half * (h + 1), :, at], 0, 1)
            for t in range(2):
                left_out[t, half * h : half * (h + 1), at] = parts[t] * keep
            return carry

        lax.fori_loop(0, x.shape[2] // chunk, step, 0)


def own_kernel(left, rows, labels, message, partial, acc, sums):
    chunk = chunk_of(left.shape[2])
    limits = first_limit + limit_step * lax.broadcasted_iota(jnp.int32, (class_count, 1), 0)
    limits = limits.astype(f32)
    acc[...] = jnp.zeros(acc.shape, f32)
    sums[...] = jnp.zeros(sums.shape, f32)

    def step(i, carry):
        at = pl.ds(pl.multiple_of(i * chunk, chunk), chunk)
        weights = rows[0:1, at].astype(bf16)
        table = jnp.where(rows[1:2, at] <= limits, rows[0:1, at], 0.0).astype(bf16)
        parts = [left[t, :, at] for t in range(2)]
        wide = [part.astype(f32) for part in parts]
        power = (wide[0] * wide[0] + wide[1] * wide[1]).astype(bf16)
        sums[...] += contract(table, power)
        acc[...] += contract(parts[0] * weights, parts[0]) + contract(parts[1] * weights, parts[1])
        return carry

    lax.fori_loop(0, left.shape[2] // chunk, step, 0)
    parts, height = message.shape[0], message.shape[1] - class_count
    for q in range(parts):
        message[q, 0:height, :] = acc[height * q : height * (q + 1), :]
        message[q, height:, :] = sums[...]
    partial[0:class_count, :] = sums[...]
    partial[class_count:, :] = jnp.broadcast_to(labels[...].astype(f32), sums.shape)


def norms(own_sums, own_labels, slice_sums, slice_labels, total):
    left_norm = jnp.zeros((slice_sums.shape[0], own_sums.shape[1]), f32)
    right_norm = left_norm
    for c in range(class_count):
        left_norm = jnp.where(slice_labels == c, own_sums[c : c + 1, :], left_norm)
        right_norm = jnp.where(own_labels == c, slice_sums[:, c : c + 1], right_norm)
    return lax.rsqrt((left_norm / total + epsilon) * (right_norm / total + epsilon)) / math.sqrt(
        total
    )


def sliced(place, height, sums, labels, scratch):
    scratch[:, 0:class_count] = sums.T
    scratch[:, class_count : 2 * class_count] = jnp.broadcast_to(
        labels, (class_count, labels.shape[1])
    ).T
    part = scratch[pl.ds(pl.multiple_of(place[0] * height, 8), height), :]
    return part[:, 0:class_count], part[:, class_count : class_count + 1]


def summed_of(message):
    summed = message[0]
    for q in range(1, message.shape[0]):
        summed = summed + message[q]
    return summed


def self_kernel(total, place, message, labels, sums_out, out, scratch):
    height = message.shape[1] - class_count
    summed = summed_of(message)
    sums = summed[height:, :]
    own_labels = labels[...].astype(f32)
    sums_out[...] = sums
    slice_sums, slice_labels = sliced(place, height, sums, own_labels, scratch)
    out[...] = summed[0:height, :] * norms(sums, own_labels, slice_sums, slice_labels, total)


def pair_kernel(first, second, rows, left, own_out, first_out, second_out, blocks, sems):
    count = own_out.shape[2]
    copies = [
        [
            pltpu.make_async_copy(
                block.at[t], blocks.at[t, pl.ds(count * s, count)], sems.at[2 * t + s]
            )
            for s, block in enumerate((first, second))
        ]
        for t in range(2)
    ]
    for pair in copies:
        for copy in pair:
            copy.start()
    weights = rows[0:1, :].astype(bf16)
    own_sum, sent_sum = None, None
    for t in range(2):
        for copy in copies[t]:
            copy.wait()
        other, own = blocks[t], left[t]
        own_part, sent_part = contract(other * weights, own), contract(other, own * weights)
        own_sum = own_part if own_sum is None else own_sum + own_part
        sent_sum = sent_part if sent_sum is None else sent_sum + sent_part
    half = first_out.shape[0]
    for s, out in enumerate((first_out, second_out)):
        own_out[s] = own_sum[count * s : count * (s + 1)]
        sent = sent_sum[count * s : count * (s + 1)].T
        out[:, 0:count] = sent[0:half]
        out[:, count:] = sent[half:]


def merge_kernel(own, first, second, first_partial, second_partial, out):
    parts, height = out.shape[0], out.shape[1] - class_count
    count = own.shape[2]
    for s, (received, partial) in enumerate(((first, first_partial), (second, second_partial))):
        half = received.shape[0]
        across = slice(count * s, count * (s + 1))
        for q in range(parts):
            side, at = divmod(q * height, half)
            out[q, 0:height, across] = (
                own[s, height * q : height * (q + 1), :]
                + received[at : at + height, count * side : count * (side + 1)]
            )
            out[q, height:, across] = partial[0:class_count, :]


def last_kernel(
    total, flag, place, pieces, sums, labels, first_partial, second_partial, self_out, out, scratch
):
    count, height = out.shape[2], out.shape[1]
    summed = summed_of(pieces)
    own_labels = labels[...].astype(f32)
    out[0] = self_out[...]
    for s, partial in enumerate((first_partial, second_partial)):
        mine = summed[:, count * s : count * (s + 1)]
        slice_sums, slice_labels = sliced(
            place, height, mine[height:, :], partial[class_count : class_count + 1, :], scratch
        )
        out[1 + (s ^ flag[0])] = mine[0:height, :] * norms(
            sums[...], own_labels, slice_sums, slice_labels, total
        )


def body(particles, classes, plan, voxel_shell, voxel_angle, shell_gain):
    blocks, voxes = lax.axis_size("blk"), lax.axis_size("vox")
    bit_count = blocks.bit_length() - 1
    count, _, width = particles.shape
    height, total = count // voxes, width * voxes
    axes = ("blk", "vox")
    bit_pairs = [(low, high) for high in range(bit_count) for low in range(high)]

    def mask_call(*refs):
        mask_kernel(bit_count, *refs)

    def self_call(*refs):
        self_kernel(total, *refs)

    def last_call(*refs):
        last_kernel(total, *refs)

    place = lax.axis_index("vox").reshape(1)
    labels = classes.reshape(1, -1)
    arrays = (particles, classes, plan, voxel_shell, voxel_angle, shell_gain)
    spaces = (pltpu.VMEM, pltpu.VMEM, pltpu.SMEM, pltpu.VMEM, pltpu.VMEM, pltpu.SMEM)
    index, flag, left, rows = local_call(
        mask_call,
        (
            shape((1,), jnp.int32),
            shape((1,), jnp.int32),
            shape((2, count, width), bf16),
            shape((8, width), f32),
        ),
        [in_hbm] * len(arrays),
        (in_smem, in_smem, in_vmem, in_vmem),
        arrays,
        [space(array.shape, array.dtype) for space, array in zip(spaces, arrays)]
        + [pltpu.SemaphoreType.DMA((1 + len(arrays),))],
        front_vmem,
    )
    index = index[0]
    scratch = [pltpu.VMEM((count, 2 * class_count), f32)]

    def fetch(bits):
        pairs = [one_way(blocks, voxes, bit) for bit in bits]

        def run(left, rows, labels, place):
            blocks_in = [lax.ppermute(left, axes, pair) for pair in pairs]
            message, partial = local_call(
                own_kernel,
                (
                    shape((voxes, height + class_count, count), f32),
                    shape((2 * class_count, count), f32),
                ),
                [in_vmem] * 3,
                (in_vmem, in_vmem),
                (left, rows, labels),
                [pltpu.VMEM((count, count), f32), pltpu.VMEM((class_count, count), f32)],
            )
            partials_in = [lax.ppermute(partial, "blk", both_ways(blocks, bit)) for bit in bits]
            message = lax.all_to_all(message, "vox", 0, 0, tiled=True)
            sums, self_out = local_call(
                self_call,
                (shape((class_count, count), f32), shape((height, count), f32)),
                [in_smem, in_vmem, in_vmem],
                (in_vmem, in_vmem),
                (place, message, labels),
                scratch,
            )
            return (*blocks_in, *partials_in, sums, self_out)

        return run

    def give_back(bits):
        return lambda *sent: tuple(
            lax.ppermute(part, axes, back(one_way(blocks, voxes, bit)))
            for part, bit in zip(sent, bits)
        )

    first, second, first_partial, second_partial, sums, self_out = lax.switch(
        index, [fetch(bits) for bits in bit_pairs], left, rows, labels, place
    )
    own, first_sent, second_sent = local_call(
        pair_kernel,
        (shape((2, count, count), f32),) + (shape((count // 2, 2 * count), f32),) * 2,
        [in_hbm, in_hbm, in_vmem, in_vmem],
        (in_vmem,) * 3,
        (first, second, rows, left),
        [pltpu.VMEM((2, 2 * count, width), bf16), pltpu.SemaphoreType.DMA((4,))],
    )
    first_back, second_back = lax.switch(
        index, [give_back(bits) for bits in bit_pairs], first_sent, second_sent
    )
    merged = local_call(
        merge_kernel,
        shape((voxes, height + class_count, 2 * count), f32),
        [in_vmem] * 5,
        in_vmem,
        (own, first_back, second_back, first_partial, second_partial),
    )
    pieces = lax.all_to_all(merged, "vox", 0, 0, tiled=True)
    out = local_call(
        last_call,
        shape((3, height, count), f32),
        [in_smem, in_smem] + [in_vmem] * 6,
        in_vmem,
        (flag, place, pieces, sums, labels, first_partial, second_partial, self_out),
        scratch,
    )
    return out.transpose(0, 2, 1)


def solution(mesh):
    in_specs = (P("blk", None, "vox"), P("blk"), P(), P("vox"), P("vox"), P())
    out_specs = P(None, "blk", "vox")
    return jax.shard_map(body, mesh=mesh, in_specs=in_specs, out_specs=out_specs, check_vma=False)
```

```python
import math

import jax
import jax.numpy as jnp
from jax import lax
from jax.experimental import pallas as pl
from jax.experimental.pallas import tpu as pltpu
from jax.sharding import PartitionSpec as P

first_shell = 4
first_limit = 48
limit_step = 3
class_count = 8
epsilon = 1e-05
front_vmem = 60 << 20

f32 = jnp.float32
bf16 = jnp.bfloat16
in_vmem = pl.BlockSpec(memory_space=pltpu.VMEM)
in_hbm = pl.BlockSpec(memory_space=pltpu.HBM)
in_smem = pl.BlockSpec(memory_space=pltpu.SMEM)


def shape(dims, dtype):
    return jax.ShapeDtypeStruct(dims, dtype)


def local_call(kernel, out_shape, in_specs, out_specs, args, scratch=(), vmem=40 << 20):
    return pl.pallas_call(
        kernel,
        out_shape=out_shape,
        in_specs=in_specs,
        out_specs=out_specs,
        scratch_shapes=scratch,
        compiler_params=pltpu.CompilerParams(vmem_limit_bytes=vmem),
    )(*args)


def contract(left_side, right_side):
    return lax.dot_general(
        left_side, right_side, (((1,), (1,)), ((), ())), preferred_element_type=f32
    )


def one_way(blocks, voxes, bit):
    return [
        (b * voxes + v, (b ^ 1 << bit) * voxes + v)
        for b in range(blocks)
        for v in range(voxes)
        if v & 1 == b >> bit & 1
    ]


def both_cores(blocks, voxes, bit):
    return [(b * voxes + v, (b ^ 1 << bit) * voxes + v) for b in range(blocks) for v in range(voxes)]


def sent_whole(bits):
    axis = [0 if bit == 0 else 1 if bit < 3 else 2 for bit in bits]
    return tuple(axis[0] != axis[1] and bit < 4 and bits[1] != 4 for bit in bits)


def back(pairs):
    return [(target, source) for source, target in pairs]


def both_ways(blocks, bit):
    return [(b, b ^ 1 << bit) for b in range(blocks)]


def column(row):
    return jnp.broadcast_to(row, (8, row.shape[1])).T[:, 0:1]


def limits_of(labels):
    return first_limit + 1.0 + limit_step * column(labels.astype(f32))


def chunk_of(width):
    return next(size for size in (256, 128, width) if width % size == 0)


def mask_kernel(
    bit_count, x, labels, plan, shells, angles, gain, index_out, flag_out, left_out, *scratch
):
    rows, buffers, sems = scratch[0], scratch[1:-1], scratch[-1]
    half = left_out.shape[1] // 2
    block, labels_in, plan_in, shells_in, angles_in, gain_in = buffers
    halves = [
        pltpu.make_async_copy(
            x.at[pl.ds(half * h, half)], block.at[pl.ds(half * h, half)], sems.at[h]
        )
        for h in range(2)
    ]
    small = [
        pltpu.make_async_copy(source, buffer, sems.at[2 + i])
        for i, (source, buffer) in enumerate(
            zip((labels, plan, shells, angles, gain), buffers[1:])
        )
    ]
    for copy in small + halves:
        copy.start()
    for copy in small:
        copy.wait()

    def bit_of(value):
        return sum([jnp.where(value >= 1 << k, 1, 0) for k in range(1, bit_count)])

    first, second = bit_of(plan_in[0, 0]), bit_of(plan_in[1, 0])
    low, high = jnp.minimum(first, second), jnp.maximum(first, second)
    index_out[0] = high * (high - 1) // 2 + low
    flag_out[0] = jnp.where(first > second, 1, 0)

    shell_row = shells_in[...].reshape(1, -1)
    angle_row = angles_in[...].reshape(1, -1).astype(f32)
    weights = jnp.zeros(shell_row.shape, f32)
    for s in range(gain.shape[0]):
        weights = jnp.where(shell_row == s + first_shell, gain_in[s], weights)
    rows[0:1, :] = weights.astype(bf16).astype(f32)
    rows[1:2, :] = angle_row
    limits = limits_of(labels_in[...].reshape(1, -1)).astype(bf16)
    chunk = chunk_of(x.shape[2])
    for h in range(2):
        halves[h].wait()

        def step(i, carry):
            at = pl.ds(pl.multiple_of(i * chunk, chunk), chunk)
            keep = jnp.clip(
                limits[half * h : half * (h + 1)] - rows[1:2, at].astype(bf16), 0, 1
            )
            parts = jnp.swapaxes(block[half * h : half * (h + 1), :, at], 0, 1)
            for t in range(2):
                left_out[t, half * h : half * (h + 1), at] = parts[t] * keep
            return carry

        lax.fori_loop(0, x.shape[2] // chunk, step, 0)


def own_kernel(left, rows, labels, message, partial, acc, sums):
    chunk = chunk_of(left.shape[2])
    limits = first_limit + limit_step * lax.broadcasted_iota(jnp.int32, (class_count, 1), 0)
    limits = limits.astype(f32)
    acc[...] = jnp.zeros(acc.shape, f32)
    sums[...] = jnp.zeros(sums.shape, f32)

    def step(i, carry):
        at = pl.ds(pl.multiple_of(i * chunk, chunk), chunk)
        weights = rows[0:1, at].astype(bf16)
        table = jnp.where(rows[1:2, at] <= limits, rows[0:1, at], 0.0).astype(bf16)
        parts = [left[t, :, at] for t in range(2)]
        wide = [part.astype(f32) for part in parts]
        power = (wide[0] * wide[0] + wide[1] * wide[1]).astype(bf16)
        sums[...] += contract(table, power)
        acc[...] += contract(parts[0] * weights, parts[0]) + contract(parts[1] * weights, parts[1])
        return carry

    lax.fori_loop(0, left.shape[2] // chunk, step, 0)
    parts, height = message.shape[0], message.shape[1] - class_count
    for q in range(parts):
        message[q, 0:height, :] = acc[height * q : height * (q + 1), :]
        message[q, height:, :] = sums[...]
    partial[0:class_count, :] = sums[...]
    partial[class_count:, :] = jnp.broadcast_to(labels[...].astype(f32), sums.shape)


def norms(own_sums, own_labels, slice_sums, slice_labels, total):
    left_norm = jnp.zeros((slice_sums.shape[0], own_sums.shape[1]), f32)
    right_norm = left_norm
    for c in range(class_count):
        left_norm = jnp.where(slice_labels == c, own_sums[c : c + 1, :], left_norm)
        right_norm = jnp.where(own_labels == c, slice_sums[:, c : c + 1], right_norm)
    return lax.rsqrt((left_norm / total + epsilon) * (right_norm / total + epsilon)) / math.sqrt(
        total
    )


def sliced(place, height, sums, labels, scratch):
    scratch[:, 0:class_count] = sums.T
    scratch[:, class_count : 2 * class_count] = jnp.broadcast_to(
        labels, (class_count, labels.shape[1])
    ).T
    part = scratch[pl.ds(pl.multiple_of(place[0] * height, 8), height), :]
    return part[:, 0:class_count], part[:, class_count : class_count + 1]


def summed_of(message):
    summed = message[0]
    for q in range(1, message.shape[0]):
        summed = summed + message[q]
    return summed


def self_kernel(total, place, message, labels, sums_out, out, scratch):
    height = message.shape[1] - class_count
    summed = summed_of(message)
    sums = summed[height:, :]
    own_labels = labels[...].astype(f32)
    sums_out[...] = sums
    slice_sums, slice_labels = sliced(place, height, sums, own_labels, scratch)
    out[...] = summed[0:height, :] * norms(sums, own_labels, slice_sums, slice_labels, total)


def pair_kernel(first, second, rows, left, own_out, first_out, second_out, blocks, sems):
    count = own_out.shape[2]
    copies = [
        [
            pltpu.make_async_copy(
                block.at[t], blocks.at[t, pl.ds(count * s, count)], sems.at[2 * t + s]
            )
            for s, block in enumerate((first, second))
        ]
        for t in range(2)
    ]
    for pair in copies:
        for copy in pair:
            copy.start()
    weights = rows[0:1, :].astype(bf16)
    own_sum, sent_sum = None, None
    for t in range(2):
        for copy in copies[t]:
            copy.wait()
        other, own = blocks[t], left[t]
        own_part, sent_part = contract(other * weights, own), contract(other, own * weights)
        own_sum = own_part if own_sum is None else own_sum + own_part
        sent_sum = sent_part if sent_sum is None else sent_sum + sent_part
    half = first_out.shape[0]
    for s, out in enumerate((first_out, second_out)):
        own_out[s] = own_sum[count * s : count * (s + 1)]
        sent = sent_sum[count * s : count * (s + 1)].T
        out[:, 0:count] = sent[0:half]
        out[:, count:] = sent[half:]


def merge_kernel(whole, own, first_partial, second_partial, *refs):
    received, out = list(refs[:-1]), refs[-1]
    parts, height = out.shape[0], out.shape[1] - class_count
    count = own.shape[2]
    for s, partial in enumerate((first_partial, second_partial)):
        back_in = None if whole[s] else received.pop(0)
        across = slice(count * s, count * (s + 1))
        for q in range(parts):
            scores = own[s, height * q : height * (q + 1), :]
            if back_in is not None:
                side, at = divmod(q * height, back_in.shape[0])
                scores += back_in[at : at + height, count * side : count * (side + 1)]
            out[q, 0:height, across] = scores
            out[q, height:, across] = partial[0:class_count, :]


def left_kernel(total, place, sums, labels, first_partial, second_partial, self_out, out, scratch):
    count, height = out.shape[2], out.shape[1]
    out[0] = self_out[...]
    for s, partial in enumerate((first_partial, second_partial)):
        scratch[...] = partial[class_count:, :].T
        part = scratch[pl.ds(pl.multiple_of(place[0] * height, 8), height), 0:1]
        norm = jnp.zeros((height, count), f32)
        for c in range(class_count):
            norm = jnp.where(part == c, sums[c : c + 1, :], norm)
        out[1 + s] = lax.rsqrt(norm / total + epsilon) / math.sqrt(total)


def last_kernel(total, flag, place, pieces, factors, labels, out, scratch):
    count, height = out.shape[2], out.shape[1]
    summed = summed_of(pieces)
    own_labels = labels[...]
    out[0] = factors[0]
    for s in range(2):
        scratch[:, class_count * s : class_count * (s + 1)] = summed[
            height:, count * s : count * (s + 1)
        ].T
    part = scratch[pl.ds(pl.multiple_of(place[0] * height, 8), height), :]
    for s in range(2):
        norm = jnp.zeros((height, count), f32)
        for c in range(class_count):
            at = class_count * s + c
            norm = jnp.where(own_labels == c, part[:, at : at + 1], norm)
        out[1 + (s ^ flag[0])] = (
            summed[0:height, count * s : count * (s + 1)]
            * factors[1 + s]
            * lax.rsqrt(norm / total + epsilon)
        )


def body(particles, classes, plan, voxel_shell, voxel_angle, shell_gain):
    blocks, voxes = lax.axis_size("blk"), lax.axis_size("vox")
    bit_count = blocks.bit_length() - 1
    count, _, width = particles.shape
    height, total = count // voxes, width * voxes
    axes = ("blk", "vox")
    bit_pairs = [(low, high) for high in range(bit_count) for low in range(high)]

    def mask_call(*refs):
        mask_kernel(bit_count, *refs)

    def self_call(*refs):
        self_kernel(total, *refs)

    def left_call(*refs):
        left_kernel(total, *refs)

    def last_call(*refs):
        last_kernel(total, *refs)

    place = lax.axis_index("vox").reshape(1)
    labels = classes.reshape(1, -1)
    arrays = (particles, classes, plan, voxel_shell, voxel_angle, shell_gain)
    spaces = (pltpu.VMEM, pltpu.VMEM, pltpu.SMEM, pltpu.VMEM, pltpu.VMEM, pltpu.SMEM)
    index, flag, left, rows = local_call(
        mask_call,
        (
            shape((1,), jnp.int32),
            shape((1,), jnp.int32),
            shape((2, count, width), bf16),
            shape((8, width), f32),
        ),
        [in_hbm] * len(arrays),
        (in_smem, in_smem, in_vmem, in_vmem),
        arrays,
        [space(array.shape, array.dtype) for space, array in zip(spaces, arrays)]
        + [pltpu.SemaphoreType.DMA((1 + len(arrays),))],
        front_vmem,
    )
    index = index[0]
    scratch = [pltpu.VMEM((count, 2 * class_count), f32)]

    def fetch(bits):
        pairs = [
            (both_cores if whole else one_way)(blocks, voxes, bit)
            for bit, whole in zip(bits, sent_whole(bits))
        ]

        def run(left, rows, labels, place):
            blocks_in = [lax.ppermute(left, axes, pair) for pair in pairs]
            message, partial = local_call(
                own_kernel,
                (
                    shape((voxes, height + class_count, count), f32),
                    shape((2 * class_count, count), f32),
                ),
                [in_vmem] * 3,
                (in_vmem, in_vmem),
                (left, rows, labels),
                [pltpu.VMEM((count, count), f32), pltpu.VMEM((class_count, count), f32)],
            )
            partials_in = [lax.ppermute(partial, "blk", both_ways(blocks, bit)) for bit in bits]
            message = lax.all_to_all(message, "vox", 0, 0, tiled=True)
            sums, self_out = local_call(
                self_call,
                (shape((class_count, count), f32), shape((height, count), f32)),
                [in_smem, in_vmem, in_vmem],
                (in_vmem, in_vmem),
                (place, message, labels),
                scratch,
            )
            return (*blocks_in, *partials_in, sums, self_out)

        return run

    def give_back(bits):
        whole = sent_whole(bits)

        def merge_call(*refs):
            merge_kernel(whole, *refs)

        def run(own, first_partial, second_partial, *sent):
            received = [
                lax.ppermute(part, axes, back(one_way(blocks, voxes, bit)))
                for part, bit, all_sent in zip(sent, bits, whole)
                if not all_sent
            ]
            return local_call(
                merge_call,
                shape((voxes, height + class_count, 2 * count), f32),
                [in_vmem] * (3 + len(received)),
                in_vmem,
                (own, first_partial, second_partial, *received),
            )

        return run

    first, second, first_partial, second_partial, sums, self_out = lax.switch(
        index, [fetch(bits) for bits in bit_pairs], left, rows, labels, place
    )
    own, first_sent, second_sent = local_call(
        pair_kernel,
        (shape((2, count, count), f32),) + (shape((count // 2, 2 * count), f32),) * 2,
        [in_hbm, in_hbm, in_vmem, in_vmem],
        (in_vmem,) * 3,
        (first, second, rows, left),
        [pltpu.VMEM((2, 2 * count, width), bf16), pltpu.SemaphoreType.DMA((4,))],
    )
    merged = lax.switch(
        index,
        [give_back(bits) for bits in bit_pairs],
        own,
        first_partial,
        second_partial,
        first_sent,
        second_sent,
    )
    pieces = lax.all_to_all(merged, "vox", 0, 0, tiled=True)
    factors = local_call(
        left_call,
        shape((3, height, count), f32),
        [in_smem] + [in_vmem] * 5,
        in_vmem,
        (place, sums, labels, first_partial, second_partial, self_out),
        [pltpu.VMEM((count, class_count), f32)],
    )
    out = local_call(
        last_call,
        shape((3, height, count), f32),
        [in_smem, in_smem] + [in_vmem] * 3,
        in_vmem,
        (flag, place, pieces, factors, labels),
        scratch,
    )
    return out.transpose(0, 2, 1)


def solution(mesh):
    in_specs = (P("blk", None, "vox"), P("blk"), P(), P("vox"), P("vox"), P())
    out_specs = P(None, "blk", "vox")
    return jax.shard_map(body, mesh=mesh, in_specs=in_specs, out_specs=out_specs, check_vma=False)
```

```python
import math

import jax
import jax.numpy as jnp
from jax import lax
from jax.experimental import pallas as pl
from jax.experimental.pallas import tpu as pltpu
from jax.sharding import PartitionSpec as P

first_shell = 4
first_limit = 48
limit_step = 3
class_count = 8
epsilon = 1e-05
front_vmem = 60 << 20

f32 = jnp.float32
bf16 = jnp.bfloat16
in_vmem = pl.BlockSpec(memory_space=pltpu.VMEM)
in_hbm = pl.BlockSpec(memory_space=pltpu.HBM)
in_smem = pl.BlockSpec(memory_space=pltpu.SMEM)


def shape(dims, dtype):
    return jax.ShapeDtypeStruct(dims, dtype)


def local_call(kernel, out_shape, in_specs, out_specs, args, scratch=(), vmem=40 << 20):
    return pl.pallas_call(
        kernel,
        out_shape=out_shape,
        in_specs=in_specs,
        out_specs=out_specs,
        scratch_shapes=scratch,
        compiler_params=pltpu.CompilerParams(vmem_limit_bytes=vmem),
    )(*args)


def contract(left_side, right_side):
    return lax.dot_general(
        left_side, right_side, (((1,), (1,)), ((), ())), preferred_element_type=f32
    )


def one_way(blocks, voxes, bit):
    return [
        (b * voxes + v, (b ^ 1 << bit) * voxes + v)
        for b in range(blocks)
        for v in range(voxes)
        if v & 1 == b >> bit & 1
    ]


def both_cores(blocks, voxes, bit):
    return [(b * voxes + v, (b ^ 1 << bit) * voxes + v) for b in range(blocks) for v in range(voxes)]


def sent_whole(bits):
    axis = [0 if bit == 0 else 1 if bit < 3 else 2 for bit in bits]
    return tuple(axis[0] != axis[1] and bit < 4 and bits[1] != 4 for bit in bits)


def back(pairs):
    return [(target, source) for source, target in pairs]


def both_ways(blocks, bit):
    return [(b, b ^ 1 << bit) for b in range(blocks)]


def column(row):
    return jnp.broadcast_to(row, (8, row.shape[1])).T[:, 0:1]


def limits_of(labels):
    return first_limit + 1.0 + limit_step * column(labels.astype(f32))


def chunk_of(width):
    return next(size for size in (256, 128, width) if width % size == 0)


def mask_kernel(
    bit_count, x, labels, plan, shells, angles, gain, index_out, flag_out, left_out, rows, labels_out, *scratch
):
    buffers, sems = scratch[:-1], scratch[-1]
    half = left_out.shape[1] // 2
    block, labels_in, plan_in, shells_in, angles_in, gain_in = buffers
    halves = [
        pltpu.make_async_copy(
            x.at[pl.ds(half * h, half)], block.at[pl.ds(half * h, half)], sems.at[h]
        )
        for h in range(2)
    ]
    small = [
        pltpu.make_async_copy(source, buffer, sems.at[2 + i])
        for i, (source, buffer) in enumerate(
            zip((labels, plan, shells, angles, gain), buffers[1:])
        )
    ]
    for copy in small + halves:
        copy.start()
    for copy in small:
        copy.wait()

    def bit_of(value):
        return sum([jnp.where(value >= 1 << k, 1, 0) for k in range(1, bit_count)])

    first, second = bit_of(plan_in[0, 0]), bit_of(plan_in[1, 0])
    low, high = jnp.minimum(first, second), jnp.maximum(first, second)
    index_out[0] = high * (high - 1) // 2 + low
    flag_out[0] = jnp.where(first > second, 1, 0)

    shell_row = shells_in[...].reshape(1, -1)
    angle_row = angles_in[...].reshape(1, -1).astype(f32)
    weights = jnp.zeros(shell_row.shape, f32)
    for s in range(gain.shape[0]):
        weights = jnp.where(shell_row == s + first_shell, gain_in[s], weights)
    rows[0:1, :] = weights.astype(bf16).astype(f32)
    rows[1:2, :] = angle_row
    labels_out[...] = labels_in[...].reshape(1, -1)
    limits = limits_of(labels_out[...]).astype(bf16)
    angle_row = angle_row.astype(bf16)
    for h in range(2):
        halves[h].wait()
        down = slice(half * h, half * (h + 1))
        keep = jnp.clip(limits[down] - angle_row, 0, 1)
        parts = jnp.swapaxes(block[down], 0, 1)
        for t in range(2):
            left_out[t, down, :] = parts[t] * keep


def own_kernel(left, rows, labels, message, partial, acc, sums):
    chunk = chunk_of(left.shape[2])
    limits = first_limit + limit_step * lax.broadcasted_iota(jnp.int32, (class_count, 1), 0)
    limits = limits.astype(f32)
    acc[...] = jnp.zeros(acc.shape, f32)
    sums[...] = jnp.zeros(sums.shape, f32)

    def step(i, carry):
        at = pl.ds(pl.multiple_of(i * chunk, chunk), chunk)
        weights = rows[0:1, at].astype(bf16)
        table = jnp.where(rows[1:2, at] <= limits, rows[0:1, at], 0.0).astype(bf16)
        parts = [left[t, :, at] for t in range(2)]
        wide = [part.astype(f32) for part in parts]
        power = (wide[0] * wide[0] + wide[1] * wide[1]).astype(bf16)
        sums[...] += contract(table, power)
        acc[...] += contract(parts[0] * weights, parts[0]) + contract(parts[1] * weights, parts[1])
        return carry

    lax.fori_loop(0, left.shape[2] // chunk, step, 0)
    parts, height = message.shape[0], message.shape[1] - class_count
    for q in range(parts):
        message[q, 0:height, :] = acc[height * q : height * (q + 1), :]
        message[q, height:, :] = sums[...]
    partial[0:class_count, :] = sums[...]
    partial[class_count:, :] = jnp.broadcast_to(labels[...].astype(f32), sums.shape)


def norms(own_sums, own_labels, slice_sums, slice_labels, total):
    left_norm = jnp.zeros((slice_sums.shape[0], own_sums.shape[1]), f32)
    right_norm = left_norm
    for c in range(class_count):
        left_norm = jnp.where(slice_labels == c, own_sums[c : c + 1, :], left_norm)
        right_norm = jnp.where(own_labels == c, slice_sums[:, c : c + 1], right_norm)
    return lax.rsqrt((left_norm / total + epsilon) * (right_norm / total + epsilon)) / math.sqrt(
        total
    )


def sliced(place, height, sums, labels, scratch):
    scratch[:, 0:class_count] = sums.T
    scratch[:, class_count : 2 * class_count] = jnp.broadcast_to(
        labels, (class_count, labels.shape[1])
    ).T
    part = scratch[pl.ds(pl.multiple_of(place[0] * height, 8), height), :]
    return part[:, 0:class_count], part[:, class_count : class_count + 1]


def summed_of(message):
    summed = message[0]
    for q in range(1, message.shape[0]):
        summed = summed + message[q]
    return summed


def self_kernel(total, place, message, labels, sums_out, out, scratch):
    height = message.shape[1] - class_count
    summed = summed_of(message)
    sums = summed[height:, :]
    own_labels = labels[...].astype(f32)
    sums_out[...] = sums
    slice_sums, slice_labels = sliced(place, height, sums, own_labels, scratch)
    out[...] = summed[0:height, :] * norms(sums, own_labels, slice_sums, slice_labels, total)


def pair_kernel(first, second, rows, left, own_out, first_out, second_out, blocks, sems):
    count = own_out.shape[2]
    copies = [
        [
            pltpu.make_async_copy(
                block.at[t], blocks.at[t, pl.ds(count * s, count)], sems.at[2 * t + s]
            )
            for s, block in enumerate((first, second))
        ]
        for t in range(2)
    ]
    for pair in copies:
        for copy in pair:
            copy.start()
    weights = rows[0:1, :].astype(bf16)
    own_sum, sent_sum = None, None
    for t in range(2):
        for copy in copies[t]:
            copy.wait()
        other, own = blocks[t], left[t]
        own_part, sent_part = contract(other * weights, own), contract(other, own * weights)
        own_sum = own_part if own_sum is None else own_sum + own_part
        sent_sum = sent_part if sent_sum is None else sent_sum + sent_part
    half = first_out.shape[0]
    for s, out in enumerate((first_out, second_out)):
        own_out[s] = own_sum[count * s : count * (s + 1)]
        sent = sent_sum[count * s : count * (s + 1)].T
        out[:, 0:count] = sent[0:half]
        out[:, count:] = sent[half:]


def merge_kernel(whole, own, first_partial, second_partial, *refs):
    received, out = list(refs[:-1]), refs[-1]
    parts, height = out.shape[0], out.shape[1] - class_count
    count = own.shape[2]
    for s, partial in enumerate((first_partial, second_partial)):
        back_in = None if whole[s] else received.pop(0)
        across = slice(count * s, count * (s + 1))
        for q in range(parts):
            scores = own[s, height * q : height * (q + 1), :]
            if back_in is not None:
                side, at = divmod(q * height, back_in.shape[0])
                scores += back_in[at : at + height, count * side : count * (side + 1)]
            out[q, 0:height, across] = scores
            out[q, height:, across] = partial[0:class_count, :]


def left_kernel(total, place, sums, labels, first_partial, second_partial, self_out, out, scratch):
    count, height = out.shape[2], out.shape[1]
    out[0] = self_out[...]
    for s, partial in enumerate((first_partial, second_partial)):
        scratch[...] = partial[class_count:, :].T
        part = scratch[pl.ds(pl.multiple_of(place[0] * height, 8), height), 0:1]
        norm = jnp.zeros((height, count), f32)
        for c in range(class_count):
            norm = jnp.where(part == c, sums[c : c + 1, :], norm)
        out[1 + s] = lax.rsqrt(norm / total + epsilon) / math.sqrt(total)


def last_kernel(total, flag, place, pieces, factors, labels, out, scratch):
    count, height = out.shape[2], out.shape[1]
    summed = summed_of(pieces)
    own_labels = labels[...]
    out[0] = factors[0]
    for s in range(2):
        scratch[:, class_count * s : class_count * (s + 1)] = summed[
            height:, count * s : count * (s + 1)
        ].T
    part = scratch[pl.ds(pl.multiple_of(place[0] * height, 8), height), :]
    for s in range(2):
        norm = jnp.zeros((height, count), f32)
        for c in range(class_count):
            at = class_count * s + c
            norm = jnp.where(own_labels == c, part[:, at : at + 1], norm)
        out[1 + (s ^ flag[0])] = (
            summed[0:height, count * s : count * (s + 1)]
            * factors[1 + s]
            * lax.rsqrt(norm / total + epsilon)
        )


def body(particles, classes, plan, voxel_shell, voxel_angle, shell_gain):
    blocks, voxes = lax.axis_size("blk"), lax.axis_size("vox")
    bit_count = blocks.bit_length() - 1
    count, _, width = particles.shape
    height, total = count // voxes, width * voxes
    axes = ("blk", "vox")
    bit_pairs = [(low, high) for high in range(bit_count) for low in range(high)]

    def mask_call(*refs):
        mask_kernel(bit_count, *refs)

    def self_call(*refs):
        self_kernel(total, *refs)

    def left_call(*refs):
        left_kernel(total, *refs)

    def last_call(*refs):
        last_kernel(total, *refs)

    place = lax.axis_index("vox").reshape(1)
    arrays = (particles, classes, plan, voxel_shell, voxel_angle, shell_gain)
    spaces = (pltpu.VMEM, pltpu.VMEM, pltpu.SMEM, pltpu.VMEM, pltpu.VMEM, pltpu.SMEM)
    index, flag, left, rows, labels = local_call(
        mask_call,
        (
            shape((1,), jnp.int32),
            shape((1,), jnp.int32),
            shape((2, count, width), bf16),
            shape((8, width), f32),
            shape((1, count), jnp.int32),
        ),
        [in_hbm] * len(arrays),
        (in_smem, in_smem) + (in_vmem,) * 3,
        arrays,
        [space(array.shape, array.dtype) for space, array in zip(spaces, arrays)]
        + [pltpu.SemaphoreType.DMA((1 + len(arrays),))],
        front_vmem,
    )
    index = index[0]
    scratch = [pltpu.VMEM((count, 2 * class_count), f32)]

    def fetch(bits):
        pairs = [
            (both_cores if whole else one_way)(blocks, voxes, bit)
            for bit, whole in zip(bits, sent_whole(bits))
        ]

        def run(left, rows, labels, place):
            blocks_in = [lax.ppermute(left, axes, pair) for pair in pairs]
            message, partial = local_call(
                own_kernel,
                (
                    shape((voxes, height + class_count, count), f32),
                    shape((2 * class_count, count), f32),
                ),
                [in_vmem] * 3,
                (in_vmem, in_vmem),
                (left, rows, labels),
                [pltpu.VMEM((count, count), f32), pltpu.VMEM((class_count, count), f32)],
            )
            partials_in = [lax.ppermute(partial, "blk", both_ways(blocks, bit)) for bit in bits]
            message = lax.all_to_all(message, "vox", 0, 0, tiled=True)
            sums, self_out = local_call(
                self_call,
                (shape((class_count, count), f32), shape((height, count), f32)),
                [in_smem, in_vmem, in_vmem],
                (in_vmem, in_vmem),
                (place, message, labels),
                scratch,
            )
            return (*blocks_in, *partials_in, sums, self_out)

        return run

    def give_back(bits):
        whole = sent_whole(bits)

        def merge_call(*refs):
            merge_kernel(whole, *refs)

        def run(own, first_partial, second_partial, *sent):
            received = [
                lax.ppermute(part, axes, back(one_way(blocks, voxes, bit)))
                for part, bit, all_sent in zip(sent, bits, whole)
                if not all_sent
            ]
            return local_call(
                merge_call,
                shape((voxes, height + class_count, 2 * count), f32),
                [in_vmem] * (3 + len(received)),
                in_vmem,
                (own, first_partial, second_partial, *received),
            )

        return run

    first, second, first_partial, second_partial, sums, self_out = lax.switch(
        index, [fetch(bits) for bits in bit_pairs], left, rows, labels, place
    )
    own, first_sent, second_sent = local_call(
        pair_kernel,
        (shape((2, count, count), f32),) + (shape((count // 2, 2 * count), f32),) * 2,
        [in_hbm, in_hbm, in_vmem, in_vmem],
        (in_vmem,) * 3,
        (first, second, rows, left),
        [pltpu.VMEM((2, 2 * count, width), bf16), pltpu.SemaphoreType.DMA((4,))],
    )
    merged = lax.switch(
        index,
        [give_back(bits) for bits in bit_pairs],
        own,
        first_partial,
        second_partial,
        first_sent,
        second_sent,
    )
    pieces = lax.all_to_all(merged, "vox", 0, 0, tiled=True)
    factors = local_call(
        left_call,
        shape((3, height, count), f32),
        [in_smem] + [in_vmem] * 5,
        in_vmem,
        (place, sums, labels, first_partial, second_partial, self_out),
        [pltpu.VMEM((count, class_count), f32)],
    )
    out = local_call(
        last_call,
        shape((3, height, count), f32),
        [in_smem, in_smem] + [in_vmem] * 3,
        in_vmem,
        (flag, place, pieces, factors, labels),
        scratch,
    )
    return out.transpose(0, 2, 1)


def solution(mesh):
    in_specs = (P("blk", None, "vox"), P("blk"), P(), P("vox"), P("vox"), P())
    out_specs = P(None, "blk", "vox")
    return jax.shard_map(body, mesh=mesh, in_specs=in_specs, out_specs=out_specs, check_vma=False)
```

```python
import math

import jax
import jax.numpy as jnp
from jax import lax
from jax.experimental import pallas as pl
from jax.experimental.pallas import tpu as pltpu
from jax.sharding import PartitionSpec as P

first_shell = 4
first_limit = 48
limit_step = 3
class_count = 8
epsilon = 1e-05
front_vmem = 60 << 20

f32 = jnp.float32
bf16 = jnp.bfloat16
in_vmem = pl.BlockSpec(memory_space=pltpu.VMEM)
in_hbm = pl.BlockSpec(memory_space=pltpu.HBM)
in_smem = pl.BlockSpec(memory_space=pltpu.SMEM)


def shape(dims, dtype):
    return jax.ShapeDtypeStruct(dims, dtype)


def local_call(kernel, out_shape, in_specs, out_specs, args, scratch=(), vmem=40 << 20):
    return pl.pallas_call(
        kernel,
        out_shape=out_shape,
        in_specs=in_specs,
        out_specs=out_specs,
        scratch_shapes=scratch,
        compiler_params=pltpu.CompilerParams(vmem_limit_bytes=vmem),
    )(*args)


def contract(left_side, right_side):
    return lax.dot_general(
        left_side, right_side, (((1,), (1,)), ((), ())), preferred_element_type=f32
    )


def one_way(blocks, voxes, bit):
    return [
        (b * voxes + v, (b ^ 1 << bit) * voxes + v)
        for b in range(blocks)
        for v in range(voxes)
        if v & 1 == b >> bit & 1
    ]


def both_cores(blocks, voxes, bit):
    return [(b * voxes + v, (b ^ 1 << bit) * voxes + v) for b in range(blocks) for v in range(voxes)]


def sent_whole(bits):
    axis = [0 if bit == 0 else 1 if bit < 3 else 2 for bit in bits]
    return tuple(axis[0] != axis[1] and bit < 4 and bits != (0, 4) for bit in bits)


def back(pairs):
    return [(target, source) for source, target in pairs]


def both_ways(blocks, bit):
    return [(b, b ^ 1 << bit) for b in range(blocks)]


def column(row):
    return jnp.broadcast_to(row, (8, row.shape[1])).T[:, 0:1]


def limits_of(labels):
    return first_limit + 1.0 + limit_step * column(labels.astype(f32))


def chunk_of(width):
    return next(size for size in (256, 128, width) if width % size == 0)


def mask_kernel(
    bit_count, x, labels, plan, shells, angles, gain, index_out, flag_out, left_out, rows, labels_out, *scratch
):
    buffers, sems = scratch[:-1], scratch[-1]
    half = left_out.shape[1] // 2
    block, labels_in, plan_in, shells_in, angles_in, gain_in = buffers
    halves = [
        pltpu.make_async_copy(
            x.at[pl.ds(half * h, half)], block.at[pl.ds(half * h, half)], sems.at[h]
        )
        for h in range(2)
    ]
    small = [
        pltpu.make_async_copy(source, buffer, sems.at[2 + i])
        for i, (source, buffer) in enumerate(
            zip((labels, plan, shells, angles, gain), buffers[1:])
        )
    ]
    for copy in small + halves:
        copy.start()
    for copy in small:
        copy.wait()

    def bit_of(value):
        return sum([jnp.where(value >= 1 << k, 1, 0) for k in range(1, bit_count)])

    first, second = bit_of(plan_in[0, 0]), bit_of(plan_in[1, 0])
    low, high = jnp.minimum(first, second), jnp.maximum(first, second)
    index_out[0] = high * (high - 1) // 2 + low
    flag_out[0] = jnp.where(first > second, 1, 0)

    shell_row = shells_in[...].reshape(1, -1)
    angle_row = angles_in[...].reshape(1, -1).astype(f32)
    weights = jnp.zeros(shell_row.shape, f32)
    for s in range(gain.shape[0]):
        weights = jnp.where(shell_row == s + first_shell, gain_in[s], weights)
    rows[0:1, :] = weights.astype(bf16).astype(f32)
    rows[1:2, :] = angle_row
    labels_out[...] = labels_in[...].reshape(1, -1)
    limits = limits_of(labels_out[...]).astype(bf16)
    angle_row = angle_row.astype(bf16)
    for h in range(2):
        halves[h].wait()
        down = slice(half * h, half * (h + 1))
        keep = jnp.clip(limits[down] - angle_row, 0, 1)
        parts = jnp.swapaxes(block[down], 0, 1)
        for t in range(2):
            left_out[t, down, :] = parts[t] * keep


def own_kernel(left, rows, labels, message, partial, acc, sums):
    chunk = chunk_of(left.shape[2])
    limits = first_limit + limit_step * lax.broadcasted_iota(jnp.int32, (class_count, 1), 0)
    limits = limits.astype(f32)
    acc[...] = jnp.zeros(acc.shape, f32)
    sums[...] = jnp.zeros(sums.shape, f32)

    def step(i, carry):
        at = pl.ds(pl.multiple_of(i * chunk, chunk), chunk)
        weights = rows[0:1, at].astype(bf16)
        table = jnp.where(rows[1:2, at] <= limits, rows[0:1, at], 0.0).astype(bf16)
        parts = [left[t, :, at] for t in range(2)]
        wide = [part.astype(f32) for part in parts]
        power = (wide[0] * wide[0] + wide[1] * wide[1]).astype(bf16)
        sums[...] += contract(table, power)
        acc[...] += contract(parts[0] * weights, parts[0]) + contract(parts[1] * weights, parts[1])
        return carry

    lax.fori_loop(0, left.shape[2] // chunk, step, 0)
    parts, height = message.shape[0], message.shape[1] - class_count
    for q in range(parts):
        message[q, 0:height, :] = acc[height * q : height * (q + 1), :]
        message[q, height:, :] = sums[...]
    partial[0:class_count, :] = sums[...]
    partial[class_count:, :] = jnp.broadcast_to(labels[...].astype(f32), sums.shape)


def norms(own_sums, own_labels, slice_sums, slice_labels, total):
    left_norm = jnp.zeros((slice_sums.shape[0], own_sums.shape[1]), f32)
    right_norm = left_norm
    for c in range(class_count):
        left_norm = jnp.where(slice_labels == c, own_sums[c : c + 1, :], left_norm)
        right_norm = jnp.where(own_labels == c, slice_sums[:, c : c + 1], right_norm)
    return lax.rsqrt((left_norm / total + epsilon) * (right_norm / total + epsilon)) / math.sqrt(
        total
    )


def sliced(place, height, sums, labels, scratch):
    scratch[:, 0:class_count] = sums.T
    scratch[:, class_count : 2 * class_count] = jnp.broadcast_to(
        labels, (class_count, labels.shape[1])
    ).T
    part = scratch[pl.ds(pl.multiple_of(place[0] * height, 8), height), :]
    return part[:, 0:class_count], part[:, class_count : class_count + 1]


def summed_of(message):
    summed = message[0]
    for q in range(1, message.shape[0]):
        summed = summed + message[q]
    return summed


def self_kernel(total, place, message, labels, sums_out, out, scratch):
    height = message.shape[1] - class_count
    summed = summed_of(message)
    sums = summed[height:, :]
    own_labels = labels[...].astype(f32)
    sums_out[...] = sums
    slice_sums, slice_labels = sliced(place, height, sums, own_labels, scratch)
    out[...] = summed[0:height, :] * norms(sums, own_labels, slice_sums, slice_labels, total)


def pair_kernel(first, second, rows, left, own_out, first_out, second_out, blocks, sems):
    count = own_out.shape[2]
    copies = [
        [
            pltpu.make_async_copy(
                block.at[t], blocks.at[t, pl.ds(count * s, count)], sems.at[2 * t + s]
            )
            for s, block in enumerate((first, second))
        ]
        for t in range(2)
    ]
    for pair in copies:
        for copy in pair:
            copy.start()
    weights = rows[0:1, :].astype(bf16)
    own_sum, sent_sum = None, None
    for t in range(2):
        for copy in copies[t]:
            copy.wait()
        other, own = blocks[t], left[t]
        own_part, sent_part = contract(other * weights, own), contract(other, own * weights)
        own_sum = own_part if own_sum is None else own_sum + own_part
        sent_sum = sent_part if sent_sum is None else sent_sum + sent_part
    half = first_out.shape[0]
    for s, out in enumerate((first_out, second_out)):
        own_out[s] = own_sum[count * s : count * (s + 1)]
        sent = sent_sum[count * s : count * (s + 1)].T
        out[:, 0:count] = sent[0:half]
        out[:, count:] = sent[half:]


def merge_kernel(whole, own, first_partial, second_partial, *refs):
    received, out = list(refs[:-1]), refs[-1]
    parts, height = out.shape[0], out.shape[1] - class_count
    count = own.shape[2]
    for s, partial in enumerate((first_partial, second_partial)):
        back_in = None if whole[s] else received.pop(0)
        across = slice(count * s, count * (s + 1))
        for q in range(parts):
            scores = own[s, height * q : height * (q + 1), :]
            if back_in is not None:
                side, at = divmod(q * height, back_in.shape[0])
                scores += back_in[at : at + height, count * side : count * (side + 1)]
            out[q, 0:height, across] = scores
            out[q, height:, across] = partial[0:class_count, :]


def left_kernel(total, place, sums, labels, first_partial, second_partial, self_out, out, scratch):
    count, height = out.shape[2], out.shape[1]
    out[0] = self_out[...]
    for s, partial in enumerate((first_partial, second_partial)):
        scratch[...] = partial[class_count:, :].T
        part = scratch[pl.ds(pl.multiple_of(place[0] * height, 8), height), 0:1]
        norm = jnp.zeros((height, count), f32)
        for c in range(class_count):
            norm = jnp.where(part == c, sums[c : c + 1, :], norm)
        out[1 + s] = lax.rsqrt(norm / total + epsilon) / math.sqrt(total)


def last_kernel(total, flag, place, pieces, factors, labels, out, scratch):
    count, height = out.shape[2], out.shape[1]
    summed = summed_of(pieces)
    own_labels = labels[...]
    out[0] = factors[0]
    for s in range(2):
        scratch[:, class_count * s : class_count * (s + 1)] = summed[
            height:, count * s : count * (s + 1)
        ].T
    part = scratch[pl.ds(pl.multiple_of(place[0] * height, 8), height), :]
    for s in range(2):
        norm = jnp.zeros((height, count), f32)
        for c in range(class_count):
            at = class_count * s + c
            norm = jnp.where(own_labels == c, part[:, at : at + 1], norm)
        out[1 + (s ^ flag[0])] = (
            summed[0:height, count * s : count * (s + 1)]
            * factors[1 + s]
            * lax.rsqrt(norm / total + epsilon)
        )


def body(particles, classes, plan, voxel_shell, voxel_angle, shell_gain):
    blocks, voxes = lax.axis_size("blk"), lax.axis_size("vox")
    bit_count = blocks.bit_length() - 1
    count, _, width = particles.shape
    height, total = count // voxes, width * voxes
    axes = ("blk", "vox")
    bit_pairs = [(low, high) for high in range(bit_count) for low in range(high)]

    def mask_call(*refs):
        mask_kernel(bit_count, *refs)

    def self_call(*refs):
        self_kernel(total, *refs)

    def left_call(*refs):
        left_kernel(total, *refs)

    def last_call(*refs):
        last_kernel(total, *refs)

    place = lax.axis_index("vox").reshape(1)
    arrays = (particles, classes, plan, voxel_shell, voxel_angle, shell_gain)
    spaces = (pltpu.VMEM, pltpu.VMEM, pltpu.SMEM, pltpu.VMEM, pltpu.VMEM, pltpu.SMEM)
    index, flag, left, rows, labels = local_call(
        mask_call,
        (
            shape((1,), jnp.int32),
            shape((1,), jnp.int32),
            shape((2, count, width), bf16),
            shape((8, width), f32),
            shape((1, count), jnp.int32),
        ),
        [in_hbm] * len(arrays),
        (in_smem, in_smem) + (in_vmem,) * 3,
        arrays,
        [space(array.shape, array.dtype) for space, array in zip(spaces, arrays)]
        + [pltpu.SemaphoreType.DMA((1 + len(arrays),))],
        front_vmem,
    )
    index = index[0]
    scratch = [pltpu.VMEM((count, 2 * class_count), f32)]

    def fetch(bits):
        pairs = [
            (both_cores if whole else one_way)(blocks, voxes, bit)
            for bit, whole in zip(bits, sent_whole(bits))
        ]

        def run(left, rows, labels, place):
            blocks_in = [lax.ppermute(left, axes, pair) for pair in pairs]
            message, partial = local_call(
                own_kernel,
                (
                    shape((voxes, height + class_count, count), f32),
                    shape((2 * class_count, count), f32),
                ),
                [in_vmem] * 3,
                (in_vmem, in_vmem),
                (left, rows, labels),
                [pltpu.VMEM((count, count), f32), pltpu.VMEM((class_count, count), f32)],
            )
            partials_in = [lax.ppermute(partial, "blk", both_ways(blocks, bit)) for bit in bits]
            message = lax.all_to_all(message, "vox", 0, 0, tiled=True)
            sums, self_out = local_call(
                self_call,
                (shape((class_count, count), f32), shape((height, count), f32)),
                [in_smem, in_vmem, in_vmem],
                (in_vmem, in_vmem),
                (place, message, labels),
                scratch,
            )
            return (*blocks_in, *partials_in, sums, self_out)

        return run

    def give_back(bits):
        whole = sent_whole(bits)

        def merge_call(*refs):
            merge_kernel(whole, *refs)

        def run(own, first_partial, second_partial, *sent):
            received = [
                lax.ppermute(part, axes, back(one_way(blocks, voxes, bit)))
                for part, bit, all_sent in zip(sent, bits, whole)
                if not all_sent
            ]
            return local_call(
                merge_call,
                shape((voxes, height + class_count, 2 * count), f32),
                [in_vmem] * (3 + len(received)),
                in_vmem,
                (own, first_partial, second_partial, *received),
            )

        return run

    first, second, first_partial, second_partial, sums, self_out = lax.switch(
        index, [fetch(bits) for bits in bit_pairs], left, rows, labels, place
    )
    own, first_sent, second_sent = local_call(
        pair_kernel,
        (shape((2, count, count), f32),) + (shape((count // 2, 2 * count), f32),) * 2,
        [in_hbm, in_hbm, in_vmem, in_vmem],
        (in_vmem,) * 3,
        (first, second, rows, left),
        [pltpu.VMEM((2, 2 * count, width), bf16), pltpu.SemaphoreType.DMA((4,))],
    )
    merged = lax.switch(
        index,
        [give_back(bits) for bits in bit_pairs],
        own,
        first_partial,
        second_partial,
        first_sent,
        second_sent,
    )
    pieces = lax.all_to_all(merged, "vox", 0, 0, tiled=True)
    factors = local_call(
        left_call,
        shape((3, height, count), f32),
        [in_smem] + [in_vmem] * 5,
        in_vmem,
        (place, sums, labels, first_partial, second_partial, self_out),
        [pltpu.VMEM((count, class_count), f32)],
    )
    out = local_call(
        last_call,
        shape((3, height, count), f32),
        [in_smem, in_smem] + [in_vmem] * 3,
        in_vmem,
        (flag, place, pieces, factors, labels),
        scratch,
    )
    return out.transpose(0, 2, 1)


def solution(mesh):
    in_specs = (P("blk", None, "vox"), P("blk"), P(), P("vox"), P("vox"), P())
    out_specs = P(None, "blk", "vox")
    return jax.shard_map(body, mesh=mesh, in_specs=in_specs, out_specs=out_specs, check_vma=False)
```

```python
import math

import jax
import jax.numpy as jnp
from jax import lax
from jax.experimental import pallas as pl
from jax.experimental.pallas import tpu as pltpu
from jax.sharding import PartitionSpec as P

first_shell = 4
first_limit = 48
limit_step = 3
class_count = 8
epsilon = 1e-05
front_vmem = 60 << 20

f32 = jnp.float32
bf16 = jnp.bfloat16
in_vmem = pl.BlockSpec(memory_space=pltpu.VMEM)
in_hbm = pl.BlockSpec(memory_space=pltpu.HBM)
in_smem = pl.BlockSpec(memory_space=pltpu.SMEM)


def shape(dims, dtype):
    return jax.ShapeDtypeStruct(dims, dtype)


def local_call(kernel, out_shape, in_specs, out_specs, args, scratch=(), vmem=40 << 20):
    return pl.pallas_call(
        kernel,
        out_shape=out_shape,
        in_specs=in_specs,
        out_specs=out_specs,
        scratch_shapes=scratch,
        compiler_params=pltpu.CompilerParams(vmem_limit_bytes=vmem),
    )(*args)


def contract(left_side, right_side):
    return lax.dot_general(
        left_side, right_side, (((1,), (1,)), ((), ())), preferred_element_type=f32
    )


def one_way(blocks, voxes, bit):
    return [
        (b * voxes + v, (b ^ 1 << bit) * voxes + v)
        for b in range(blocks)
        for v in range(voxes)
        if v & 1 == b >> bit & 1
    ]


def both_cores(blocks, voxes, bit):
    return [(b * voxes + v, (b ^ 1 << bit) * voxes + v) for b in range(blocks) for v in range(voxes)]


def sent_whole(bits):
    axis = [0 if bit == 0 else 1 if bit < 3 else 2 for bit in bits]
    return tuple(axis[0] != axis[1] and bit < 4 and bits != (0, 4) for bit in bits)


def back(pairs):
    return [(target, source) for source, target in pairs]


def both_ways(blocks, bit):
    return [(b, b ^ 1 << bit) for b in range(blocks)]


def column(row):
    return jnp.broadcast_to(row, (8, row.shape[1])).T[:, 0:1]


def limits_of(labels):
    return first_limit + 1.0 + limit_step * column(labels.astype(f32))


def chunk_of(width):
    return next(size for size in (256, 128, width) if width % size == 0)


def mask_kernel(
    bit_count, x, labels, plan, shells, angles, gain, index_out, flag_out, left_out, rows, labels_out, *scratch
):
    buffers, sems = scratch[:-1], scratch[-1]
    half = left_out.shape[1] // 2
    block, labels_in, plan_in, shells_in, angles_in, gain_in = buffers
    halves = [
        pltpu.make_async_copy(
            x.at[pl.ds(half * h, half)], block.at[pl.ds(half * h, half)], sems.at[h]
        )
        for h in range(2)
    ]
    small = [
        pltpu.make_async_copy(source, buffer, sems.at[2 + i])
        for i, (source, buffer) in enumerate(
            zip((labels, plan, shells, angles, gain), buffers[1:])
        )
    ]
    for copy in small + halves:
        copy.start()
    for copy in small:
        copy.wait()

    def bit_of(value):
        return sum([jnp.where(value >= 1 << k, 1, 0) for k in range(1, bit_count)])

    first, second = bit_of(plan_in[0, 0]), bit_of(plan_in[1, 0])
    low, high = jnp.minimum(first, second), jnp.maximum(first, second)
    index_out[0] = high * (high - 1) // 2 + low
    flag_out[0] = jnp.where(first > second, 1, 0)

    shell_row = shells_in[...].reshape(1, -1)
    angle_row = angles_in[...].reshape(1, -1).astype(f32)
    weights = jnp.zeros(shell_row.shape, f32)
    for s in range(gain.shape[0]):
        weights = jnp.where(shell_row == s + first_shell, gain_in[s], weights)
    rows[0:1, :] = weights.astype(bf16).astype(f32)
    rows[1:2, :] = angle_row
    labels_out[...] = labels_in[...].reshape(1, -1)
    limits = limits_of(labels_out[...]).astype(bf16)
    angle_row = angle_row.astype(bf16)
    for h in range(2):
        halves[h].wait()
        down = slice(half * h, half * (h + 1))
        keep = jnp.clip(limits[down] - angle_row, 0, 1)
        parts = jnp.swapaxes(block[down], 0, 1)
        for t in range(2):
            left_out[t, down, :] = parts[t] * keep


def own_kernel(left, rows, labels, message, partial, acc, sums):
    chunk = chunk_of(left.shape[2])
    limits = first_limit + limit_step * lax.broadcasted_iota(jnp.int32, (class_count, 1), 0)
    limits = limits.astype(f32)
    acc[...] = jnp.zeros(acc.shape, f32)
    sums[...] = jnp.zeros(sums.shape, f32)

    def step(i, carry):
        at = pl.ds(pl.multiple_of(i * chunk, chunk), chunk)
        weights = rows[0:1, at].astype(bf16)
        table = jnp.where(rows[1:2, at] <= limits, rows[0:1, at], 0.0).astype(bf16)
        parts = [left[t, :, at] for t in range(2)]
        wide = [part.astype(f32) for part in parts]
        power = (wide[0] * wide[0] + wide[1] * wide[1]).astype(bf16)
        sums[...] += contract(table, power)
        acc[...] += contract(parts[0] * weights, parts[0]) + contract(parts[1] * weights, parts[1])
        return carry

    lax.fori_loop(0, left.shape[2] // chunk, step, 0)
    parts, height = message.shape[0], message.shape[1] - class_count
    for q in range(parts):
        message[q, 0:height, :] = acc[height * q : height * (q + 1), :]
        message[q, height:, :] = sums[...]
    partial[0:class_count, :] = sums[...]
    partial[class_count:, :] = jnp.broadcast_to(labels[...].astype(f32), sums.shape)


def norms(own_sums, own_labels, slice_sums, slice_labels, total):
    left_norm = jnp.zeros((slice_sums.shape[0], own_sums.shape[1]), f32)
    right_norm = left_norm
    for c in range(class_count):
        left_norm = jnp.where(slice_labels == c, own_sums[c : c + 1, :], left_norm)
        right_norm = jnp.where(own_labels == c, slice_sums[:, c : c + 1], right_norm)
    return lax.rsqrt((left_norm / total + epsilon) * (right_norm / total + epsilon)) / math.sqrt(
        total
    )


def sliced(place, height, sums, labels, scratch):
    scratch[:, 0:class_count] = sums.T
    scratch[:, class_count : 2 * class_count] = jnp.broadcast_to(
        labels, (class_count, labels.shape[1])
    ).T
    part = scratch[pl.ds(pl.multiple_of(place[0] * height, 8), height), :]
    return part[:, 0:class_count], part[:, class_count : class_count + 1]


def summed_of(message):
    summed = message[0]
    for q in range(1, message.shape[0]):
        summed = summed + message[q]
    return summed


def self_kernel(total, place, message, labels, sums_out, out, scratch):
    height = message.shape[1] - class_count
    summed = summed_of(message)
    sums = summed[height:, :]
    own_labels = labels[...].astype(f32)
    sums_out[...] = sums
    slice_sums, slice_labels = sliced(place, height, sums, own_labels, scratch)
    out[...] = summed[0:height, :] * norms(sums, own_labels, slice_sums, slice_labels, total)


def pair_kernel(
    first,
    second,
    first_partial,
    second_partial,
    rows,
    left,
    own_out,
    first_out,
    second_out,
    table_out,
    blocks,
    tables,
    sems,
):
    count = own_out.shape[2]
    copies = [
        [
            pltpu.make_async_copy(
                block.at[t], blocks.at[t, pl.ds(count * s, count)], sems.at[2 * t + s]
            )
            for s, block in enumerate((first, second))
        ]
        for t in range(2)
    ]
    table_copies = [
        pltpu.make_async_copy(partial, tables.at[s], sems.at[4 + s])
        for s, partial in enumerate((first_partial, second_partial))
    ]
    for copy in copies[0] + table_copies + copies[1]:
        copy.start()
    weights = rows[0:1, :].astype(bf16)
    own_sum, sent_sum = None, None
    for t in range(2):
        for copy in copies[t]:
            copy.wait()
        other, own = blocks[t], left[t]
        own_part, sent_part = contract(other * weights, own), contract(other, own * weights)
        own_sum = own_part if own_sum is None else own_sum + own_part
        sent_sum = sent_part if sent_sum is None else sent_sum + sent_part
    half = first_out.shape[0]
    for s, out in enumerate((first_out, second_out)):
        own_out[s] = own_sum[count * s : count * (s + 1)]
        sent = sent_sum[count * s : count * (s + 1)].T
        out[:, 0:count] = sent[0:half]
        out[:, count:] = sent[half:]
        table_copies[s].wait()
        table_out[:, count * s : count * (s + 1)] = tables[s, 0:class_count, :]


def merge_kernel(whole, own, table, *refs):
    received, out = list(refs[:-1]), refs[-1]
    parts, height = out.shape[0], out.shape[1] - class_count
    count = own.shape[2]
    for s in range(2):
        back_in = None if whole[s] else received.pop(0)
        across = slice(count * s, count * (s + 1))
        for q in range(parts):
            scores = own[s, height * q : height * (q + 1), :]
            if back_in is not None:
                side, at = divmod(q * height, back_in.shape[0])
                scores += back_in[at : at + height, count * side : count * (side + 1)]
            out[q, 0:height, across] = scores
    for q in range(parts):
        out[q, height:, :] = table[...]


def left_kernel(total, place, sums, labels, first_partial, second_partial, self_out, out, scratch):
    count, height = out.shape[2], out.shape[1]
    out[0] = self_out[...]
    for s, partial in enumerate((first_partial, second_partial)):
        scratch[...] = partial[class_count:, :].T
        part = scratch[pl.ds(pl.multiple_of(place[0] * height, 8), height), 0:1]
        norm = jnp.zeros((height, count), f32)
        for c in range(class_count):
            norm = jnp.where(part == c, sums[c : c + 1, :], norm)
        out[1 + s] = lax.rsqrt(norm / total + epsilon) / math.sqrt(total)


def last_kernel(total, flag, place, pieces, factors, labels, out, scratch):
    count, height = out.shape[2], out.shape[1]
    summed = summed_of(pieces)
    own_labels = labels[...]
    out[0] = factors[0]
    for s in range(2):
        scratch[:, class_count * s : class_count * (s + 1)] = summed[
            height:, count * s : count * (s + 1)
        ].T
    part = scratch[pl.ds(pl.multiple_of(place[0] * height, 8), height), :]
    for s in range(2):
        norm = jnp.zeros((height, count), f32)
        for c in range(class_count):
            at = class_count * s + c
            norm = jnp.where(own_labels == c, part[:, at : at + 1], norm)
        out[1 + (s ^ flag[0])] = (
            summed[0:height, count * s : count * (s + 1)]
            * factors[1 + s]
            * lax.rsqrt(norm / total + epsilon)
        )


def body(particles, classes, plan, voxel_shell, voxel_angle, shell_gain):
    blocks, voxes = lax.axis_size("blk"), lax.axis_size("vox")
    bit_count = blocks.bit_length() - 1
    count, _, width = particles.shape
    height, total = count // voxes, width * voxes
    axes = ("blk", "vox")
    bit_pairs = [(low, high) for high in range(bit_count) for low in range(high)]

    def mask_call(*refs):
        mask_kernel(bit_count, *refs)

    def self_call(*refs):
        self_kernel(total, *refs)

    def left_call(*refs):
        left_kernel(total, *refs)

    def last_call(*refs):
        last_kernel(total, *refs)

    place = lax.axis_index("vox").reshape(1)
    arrays = (particles, classes, plan, voxel_shell, voxel_angle, shell_gain)
    spaces = (pltpu.VMEM, pltpu.VMEM, pltpu.SMEM, pltpu.VMEM, pltpu.VMEM, pltpu.SMEM)
    index, flag, left, rows, labels = local_call(
        mask_call,
        (
            shape((1,), jnp.int32),
            shape((1,), jnp.int32),
            shape((2, count, width), bf16),
            shape((8, width), f32),
            shape((1, count), jnp.int32),
        ),
        [in_hbm] * len(arrays),
        (in_smem, in_smem) + (in_vmem,) * 3,
        arrays,
        [space(array.shape, array.dtype) for space, array in zip(spaces, arrays)]
        + [pltpu.SemaphoreType.DMA((1 + len(arrays),))],
        front_vmem,
    )
    index = index[0]
    scratch = [pltpu.VMEM((count, 2 * class_count), f32)]

    def fetch(bits):
        pairs = [
            (both_cores if whole else one_way)(blocks, voxes, bit)
            for bit, whole in zip(bits, sent_whole(bits))
        ]

        def run(left, rows, labels, place):
            blocks_in = [lax.ppermute(left, axes, pair) for pair in pairs]
            message, partial = local_call(
                own_kernel,
                (
                    shape((voxes, height + class_count, count), f32),
                    shape((2 * class_count, count), f32),
                ),
                [in_vmem] * 3,
                (in_vmem, in_vmem),
                (left, rows, labels),
                [pltpu.VMEM((count, count), f32), pltpu.VMEM((class_count, count), f32)],
            )
            partials_in = [lax.ppermute(partial, "blk", both_ways(blocks, bit)) for bit in bits]
            message = lax.all_to_all(message, "vox", 0, 0, tiled=True)
            sums, self_out = local_call(
                self_call,
                (shape((class_count, count), f32), shape((height, count), f32)),
                [in_smem, in_vmem, in_vmem],
                (in_vmem, in_vmem),
                (place, message, labels),
                scratch,
            )
            return (*blocks_in, *partials_in, sums, self_out)

        return run

    def give_back(bits):
        whole = sent_whole(bits)

        def merge_call(*refs):
            merge_kernel(whole, *refs)

        def run(own, table, *sent):
            received = [
                lax.ppermute(part, axes, back(one_way(blocks, voxes, bit)))
                for part, bit, all_sent in zip(sent, bits, whole)
                if not all_sent
            ]
            return local_call(
                merge_call,
                shape((voxes, height + class_count, 2 * count), f32),
                [in_vmem] * (2 + len(received)),
                in_vmem,
                (own, table, *received),
            )

        return run

    first, second, first_partial, second_partial, sums, self_out = lax.switch(
        index, [fetch(bits) for bits in bit_pairs], left, rows, labels, place
    )
    own, first_sent, second_sent, table = local_call(
        pair_kernel,
        (shape((2, count, count), f32),)
        + (shape((count // 2, 2 * count), f32),) * 2
        + (shape((class_count, 2 * count), f32),),
        [in_hbm] * 4 + [in_vmem] * 2,
        (in_vmem,) * 4,
        (first, second, first_partial, second_partial, rows, left),
        [
            pltpu.VMEM((2, 2 * count, width), bf16),
            pltpu.VMEM((2, 2 * class_count, count), f32),
            pltpu.SemaphoreType.DMA((6,)),
        ],
    )
    merged = lax.switch(
        index, [give_back(bits) for bits in bit_pairs], own, table, first_sent, second_sent
    )
    pieces = lax.all_to_all(merged, "vox", 0, 0, tiled=True)
    factors = local_call(
        left_call,
        shape((3, height, count), f32),
        [in_smem] + [in_vmem] * 5,
        in_vmem,
        (place, sums, labels, first_partial, second_partial, self_out),
        [pltpu.VMEM((count, class_count), f32)],
    )
    out = local_call(
        last_call,
        shape((3, height, count), f32),
        [in_smem, in_smem] + [in_vmem] * 3,
        in_vmem,
        (flag, place, pieces, factors, labels),
        scratch,
    )
    return out.transpose(0, 2, 1)


def solution(mesh):
    in_specs = (P("blk", None, "vox"), P("blk"), P(), P("vox"), P("vox"), P())
    out_specs = P(None, "blk", "vox")
    return jax.shard_map(body, mesh=mesh, in_specs=in_specs, out_specs=out_specs, check_vma=False)
```

```python
import math

import jax
import jax.numpy as jnp
from jax import lax
from jax.experimental import pallas as pl
from jax.experimental.pallas import tpu as pltpu
from jax.sharding import PartitionSpec as P

first_shell = 4
first_limit = 48
limit_step = 3
class_count = 8
epsilon = 1e-05
front_vmem = 60 << 20

f32 = jnp.float32
bf16 = jnp.bfloat16
in_vmem = pl.BlockSpec(memory_space=pltpu.VMEM)
in_hbm = pl.BlockSpec(memory_space=pltpu.HBM)
in_smem = pl.BlockSpec(memory_space=pltpu.SMEM)


def shape(dims, dtype):
    return jax.ShapeDtypeStruct(dims, dtype)


def local_call(kernel, out_shape, in_specs, out_specs, args, scratch=(), vmem=40 << 20):
    return pl.pallas_call(
        kernel,
        out_shape=out_shape,
        in_specs=in_specs,
        out_specs=out_specs,
        scratch_shapes=scratch,
        compiler_params=pltpu.CompilerParams(vmem_limit_bytes=vmem),
    )(*args)


def contract(left_side, right_side):
    return lax.dot_general(
        left_side, right_side, (((1,), (1,)), ((), ())), preferred_element_type=f32
    )


def one_way(blocks, voxes, bit):
    return [
        (b * voxes + v, (b ^ 1 << bit) * voxes + v)
        for b in range(blocks)
        for v in range(voxes)
        if v & 1 == b >> bit & 1
    ]


def both_cores(blocks, voxes, bit):
    return [(b * voxes + v, (b ^ 1 << bit) * voxes + v) for b in range(blocks) for v in range(voxes)]


def sent_whole(bits):
    axis = [0 if bit == 0 else 1 if bit < 3 else 2 for bit in bits]
    return tuple(axis[0] != axis[1] and bit < 4 and bits != (0, 4) for bit in bits)


def back(pairs):
    return [(target, source) for source, target in pairs]


def both_ways(blocks, bit):
    return [(b, b ^ 1 << bit) for b in range(blocks)]


def column(row):
    return jnp.broadcast_to(row, (8, row.shape[1])).T[:, 0:1]


def limits_of(labels):
    return first_limit + 1.0 + limit_step * column(labels.astype(f32))


def chunk_of(width):
    return next(size for size in (256, 128, width) if width % size == 0)


def mask_kernel(
    bit_count, x, labels, plan, shells, angles, gain, index_out, flag_out, left_out, rows, labels_out, *scratch
):
    buffers, sems = scratch[:-1], scratch[-1]
    half = left_out.shape[1] // 2
    block, labels_in, plan_in, shells_in, angles_in, gain_in = buffers
    halves = [
        pltpu.make_async_copy(
            x.at[pl.ds(half * h, half)], block.at[pl.ds(half * h, half)], sems.at[h]
        )
        for h in range(2)
    ]
    small = [
        pltpu.make_async_copy(source, buffer, sems.at[2 + i])
        for i, (source, buffer) in enumerate(
            zip((labels, plan, shells, angles, gain), buffers[1:])
        )
    ]
    for copy in small + halves:
        copy.start()
    for copy in small:
        copy.wait()

    def bit_of(value):
        return sum([jnp.where(value >= 1 << k, 1, 0) for k in range(1, bit_count)])

    first, second = bit_of(plan_in[0, 0]), bit_of(plan_in[1, 0])
    low, high = jnp.minimum(first, second), jnp.maximum(first, second)
    index_out[0] = high * (high - 1) // 2 + low
    flag_out[0] = jnp.where(first > second, 1, 0)

    shell_row = shells_in[...].reshape(1, -1)
    angle_row = angles_in[...].reshape(1, -1).astype(f32)
    weights = jnp.zeros(shell_row.shape, f32)
    for s in range(gain.shape[0]):
        weights = jnp.where(shell_row == s + first_shell, gain_in[s], weights)
    rows[0:1, :] = weights.astype(bf16).astype(f32)
    rows[1:2, :] = angle_row
    labels_out[...] = labels_in[...].reshape(1, -1)
    limits = limits_of(labels_out[...]).astype(bf16)
    angle_row = angle_row.astype(bf16)
    for h in range(2):
        halves[h].wait()
        down = slice(half * h, half * (h + 1))
        keep = jnp.clip(limits[down] - angle_row, 0, 1)
        parts = jnp.swapaxes(block[down], 0, 1)
        for t in range(2):
            left_out[t, down, :] = parts[t] * keep


def own_kernel(left, rows, labels, message, partial, acc, sums):
    chunk = chunk_of(left.shape[2])
    limits = first_limit + limit_step * lax.broadcasted_iota(jnp.int32, (class_count, 1), 0)
    limits = limits.astype(f32)
    acc[...] = jnp.zeros(acc.shape, f32)
    sums[...] = jnp.zeros(sums.shape, f32)

    def step(i, carry):
        at = pl.ds(pl.multiple_of(i * chunk, chunk), chunk)
        weights = rows[0:1, at].astype(bf16)
        table = jnp.where(rows[1:2, at] <= limits, rows[0:1, at], 0.0).astype(bf16)
        parts = [left[t, :, at] for t in range(2)]
        wide = [part.astype(f32) for part in parts]
        power = (wide[0] * wide[0] + wide[1] * wide[1]).astype(bf16)
        sums[...] += contract(table, power)
        acc[...] += contract(parts[0] * weights, parts[0]) + contract(parts[1] * weights, parts[1])
        return carry

    lax.fori_loop(0, left.shape[2] // chunk, step, 0)
    parts, height = message.shape[0], message.shape[1] - class_count
    for q in range(parts):
        message[q, 0:height, :] = acc[height * q : height * (q + 1), :]
        message[q, height:, :] = sums[...]
    partial[0:class_count, :] = sums[...]
    partial[class_count:, :] = jnp.broadcast_to(labels[...].astype(f32), sums.shape)


def norms(own_sums, own_labels, slice_sums, slice_labels, total):
    left_norm = jnp.zeros((slice_sums.shape[0], own_sums.shape[1]), f32)
    right_norm = left_norm
    for c in range(class_count):
        left_norm = jnp.where(slice_labels == c, own_sums[c : c + 1, :], left_norm)
        right_norm = jnp.where(own_labels == c, slice_sums[:, c : c + 1], right_norm)
    return lax.rsqrt((left_norm / total + epsilon) * (right_norm / total + epsilon)) / math.sqrt(
        total
    )


def sliced(place, height, sums, labels, scratch):
    scratch[:, 0:class_count] = sums.T
    scratch[:, class_count : 2 * class_count] = jnp.broadcast_to(
        labels, (class_count, labels.shape[1])
    ).T
    part = scratch[pl.ds(pl.multiple_of(place[0] * height, 8), height), :]
    return part[:, 0:class_count], part[:, class_count : class_count + 1]


def summed_of(message):
    summed = message[0]
    for q in range(1, message.shape[0]):
        summed = summed + message[q]
    return summed


def self_kernel(total, place, message, labels, sums_out, out, scratch):
    height = message.shape[1] - class_count
    summed = summed_of(message)
    sums = summed[height:, :]
    own_labels = labels[...].astype(f32)
    sums_out[...] = sums
    slice_sums, slice_labels = sliced(place, height, sums, own_labels, scratch)
    out[...] = summed[0:height, :] * norms(sums, own_labels, slice_sums, slice_labels, total)


def pair_kernel(
    first,
    second,
    first_partial,
    second_partial,
    rows,
    left,
    own_out,
    first_out,
    second_out,
    table_out,
    blocks,
    tables,
    sems,
):
    count = own_out.shape[2]
    copies = [
        [
            pltpu.make_async_copy(
                block.at[t], blocks.at[t, pl.ds(count * s, count)], sems.at[2 * t + s]
            )
            for s, block in enumerate((first, second))
        ]
        for t in range(2)
    ]
    table_copies = [
        pltpu.make_async_copy(partial, tables.at[s], sems.at[4 + s])
        for s, partial in enumerate((first_partial, second_partial))
    ]
    for copy in copies[0] + table_copies + copies[1]:
        copy.start()
    weights = rows[0:1, :].astype(bf16)
    own_sum, sent_sum = None, None
    for t in range(2):
        for copy in copies[t]:
            copy.wait()
        other, own = blocks[t], left[t]
        own_part, sent_part = contract(other * weights, own), contract(other, own * weights)
        own_sum = own_part if own_sum is None else own_sum + own_part
        sent_sum = sent_part if sent_sum is None else sent_sum + sent_part
    half = first_out.shape[0]
    for s, out in enumerate((first_out, second_out)):
        own_out[s] = own_sum[count * s : count * (s + 1)]
        sent = sent_sum[count * s : count * (s + 1)].T
        out[:, 0:count] = sent[0:half]
        out[:, count:] = sent[half:]
        table_copies[s].wait()
        table_out[:, count * s : count * (s + 1)] = tables[s, 0:class_count, :]


def merge_kernel(whole, own, table, *refs):
    received, out = list(refs[:-1]), refs[-1]
    parts, height = out.shape[0], out.shape[1] - class_count
    count = own.shape[2]
    for s in range(2):
        back_in = None if whole[s] else received.pop(0)
        across = slice(count * s, count * (s + 1))
        for q in range(parts):
            scores = own[s, height * q : height * (q + 1), :]
            if back_in is not None:
                side, at = divmod(q * height, back_in.shape[0])
                scores += back_in[at : at + height, count * side : count * (side + 1)]
            out[q, 0:height, across] = scores
    for q in range(parts):
        out[q, height:, :] = table[...]


def left_kernel(
    total, place, flag, sums, labels, first_partial, second_partial, self_out, out, scalars, scratch
):
    count, height = out.shape[2], out.shape[1]
    scalars[0:1, :] = jnp.full((1, scalars.shape[1]), flag[0], jnp.int32)
    scalars[1:2, :] = jnp.full((1, scalars.shape[1]), place[0], jnp.int32)
    out[0] = self_out[...]
    for s, partial in enumerate((first_partial, second_partial)):
        scratch[...] = partial[class_count:, :].T
        part = scratch[pl.ds(pl.multiple_of(place[0] * height, 8), height), 0:1]
        norm = jnp.zeros((height, count), f32)
        for c in range(class_count):
            norm = jnp.where(part == c, sums[c : c + 1, :], norm)
        out[1 + s] = lax.rsqrt(norm / total + epsilon) / math.sqrt(total)


def last_kernel(total, parts, pieces, factors, labels, scalars, out):
    count, height = out.shape[2], out.shape[1]
    summed = summed_of(pieces)
    own_labels = labels[...]
    out[0] = factors[0]
    swap, place = scalars[0:1, 0:1], scalars[1:2, 0:1]
    found = []
    for s in range(2):
        sums = summed[height:, count * s : count * (s + 1)].T
        part = sums[0:height]
        for q in range(1, parts):
            part = jnp.where(place == q, sums[height * q : height * (q + 1)], part)
        norm = jnp.zeros((height, count), f32)
        for c in range(class_count):
            norm = jnp.where(own_labels == c, part[:, c : c + 1], norm)
        found.append(
            summed[0:height, count * s : count * (s + 1)]
            * factors[1 + s]
            * lax.rsqrt(norm / total + epsilon)
        )
    out[1] = jnp.where(swap == 0, found[0], found[1])
    out[2] = jnp.where(swap == 0, found[1], found[0])


def body(particles, classes, plan, voxel_shell, voxel_angle, shell_gain):
    blocks, voxes = lax.axis_size("blk"), lax.axis_size("vox")
    bit_count = blocks.bit_length() - 1
    count, _, width = particles.shape
    height, total = count // voxes, width * voxes
    axes = ("blk", "vox")
    bit_pairs = [(low, high) for high in range(bit_count) for low in range(high)]

    def mask_call(*refs):
        mask_kernel(bit_count, *refs)

    def self_call(*refs):
        self_kernel(total, *refs)

    def left_call(*refs):
        left_kernel(total, *refs)

    def last_call(*refs):
        last_kernel(total, voxes, *refs)

    place = lax.axis_index("vox").reshape(1)
    arrays = (particles, classes, plan, voxel_shell, voxel_angle, shell_gain)
    spaces = (pltpu.VMEM, pltpu.VMEM, pltpu.SMEM, pltpu.VMEM, pltpu.VMEM, pltpu.SMEM)
    index, flag, left, rows, labels = local_call(
        mask_call,
        (
            shape((1,), jnp.int32),
            shape((1,), jnp.int32),
            shape((2, count, width), bf16),
            shape((8, width), f32),
            shape((1, count), jnp.int32),
        ),
        [in_hbm] * len(arrays),
        (in_smem, in_smem) + (in_vmem,) * 3,
        arrays,
        [space(array.shape, array.dtype) for space, array in zip(spaces, arrays)]
        + [pltpu.SemaphoreType.DMA((1 + len(arrays),))],
        front_vmem,
    )
    index = index[0]
    scratch = [pltpu.VMEM((count, 2 * class_count), f32)]

    def fetch(bits):
        pairs = [
            (both_cores if whole else one_way)(blocks, voxes, bit)
            for bit, whole in zip(bits, sent_whole(bits))
        ]

        def run(left, rows, labels, place):
            blocks_in = [lax.ppermute(left, axes, pair) for pair in pairs]
            message, partial = local_call(
                own_kernel,
                (
                    shape((voxes, height + class_count, count), f32),
                    shape((2 * class_count, count), f32),
                ),
                [in_vmem] * 3,
                (in_vmem, in_vmem),
                (left, rows, labels),
                [pltpu.VMEM((count, count), f32), pltpu.VMEM((class_count, count), f32)],
            )
            partials_in = [lax.ppermute(partial, "blk", both_ways(blocks, bit)) for bit in bits]
            message = lax.all_to_all(message, "vox", 0, 0, tiled=True)
            sums, self_out = local_call(
                self_call,
                (shape((class_count, count), f32), shape((height, count), f32)),
                [in_smem, in_vmem, in_vmem],
                (in_vmem, in_vmem),
                (place, message, labels),
                scratch,
            )
            return (*blocks_in, *partials_in, sums, self_out)

        return run

    def give_back(bits):
        whole = sent_whole(bits)

        def merge_call(*refs):
            merge_kernel(whole, *refs)

        def run(own, table, *sent):
            received = [
                lax.ppermute(part, axes, back(one_way(blocks, voxes, bit)))
                for part, bit, all_sent in zip(sent, bits, whole)
                if not all_sent
            ]
            return local_call(
                merge_call,
                shape((voxes, height + class_count, 2 * count), f32),
                [in_vmem] * (2 + len(received)),
                in_vmem,
                (own, table, *received),
            )

        return run

    first, second, first_partial, second_partial, sums, self_out = lax.switch(
        index, [fetch(bits) for bits in bit_pairs], left, rows, labels, place
    )
    own, first_sent, second_sent, table = local_call(
        pair_kernel,
        (shape((2, count, count), f32),)
        + (shape((count // 2, 2 * count), f32),) * 2
        + (shape((class_count, 2 * count), f32),),
        [in_hbm] * 4 + [in_vmem] * 2,
        (in_vmem,) * 4,
        (first, second, first_partial, second_partial, rows, left),
        [
            pltpu.VMEM((2, 2 * count, width), bf16),
            pltpu.VMEM((2, 2 * class_count, count), f32),
            pltpu.SemaphoreType.DMA((6,)),
        ],
    )
    merged = lax.switch(
        index, [give_back(bits) for bits in bit_pairs], own, table, first_sent, second_sent
    )
    pieces = lax.all_to_all(merged, "vox", 0, 0, tiled=True)
    factors, scalars = local_call(
        left_call,
        (shape((3, height, count), f32), shape((8, 128), jnp.int32)),
        [in_smem] * 2 + [in_vmem] * 5,
        (in_vmem,) * 2,
        (place, flag, sums, labels, first_partial, second_partial, self_out),
        [pltpu.VMEM((count, class_count), f32)],
    )
    out = local_call(
        last_call,
        shape((3, height, count), f32),
        [in_vmem] * 4,
        in_vmem,
        (pieces, factors, labels, scalars),
    )
    return out.transpose(0, 2, 1)


def solution(mesh):
    in_specs = (P("blk", None, "vox"), P("blk"), P(), P("vox"), P("vox"), P())
    out_specs = P(None, "blk", "vox")
    return jax.shard_map(body, mesh=mesh, in_specs=in_specs, out_specs=out_specs, check_vma=False)
```
